256 devices in a mesh: section: 8 (over z), et: 32 (over x, y, core).
Axes of the slice: x: 4, y: 4, z: 8, core: 2. Of those that a mesh axis runs over, the one named last changes fastest.
Arguments:
- acts: bfloat16 [8, 512, 6144], P('section', 'et'), may hold values from -6 to 6
- norm_gain: float32 [8, 6144], P('section'), may hold values from 0.5 to 1.5
- router: bfloat16 [8, 6144, 8], P('section'), may hold values from -0.078125 to 0.078125
- w_gate: bfloat16 [8, 6144, 8192], P('section', None, 'et'), may hold values from -0.078125 to 0.078125
- w_up: bfloat16 [8, 6144, 8192], P('section', None, 'et'), may hold values from -0.078125 to 0.078125
- w_down: bfloat16 [8, 8192, 6144], P('section', 'et'), may hold values from -0.0625 to 0.0625
- expert_ids: int32 [8, 8, 512, 2], P('section', None, 'et'), may hold values from 0 to 7, as said below
Outputs:
- finished: bfloat16 [8, 512, 6144], P('section', 'et')
The draws below stay inside these ranges and needn't reach their ends.
Inputs may be any that keep to these rules, and one draw needn't show every extreme that they name: `expert_ids`: the two ids of a row differ. Of the 16 rows of one device in one micro-batch and layer, 1 to 4 name expert 0; for each layer, one micro-batch has exactly 4 such rows on every device.
All inputs are finite; a program needn't handle non-finite values.
Results may differ from the reference program's by a relative error of at most 0.014.
Values may be sent and summed in bfloat16 or wider, within the bound.
A program may use at most 64 MiB of HBM per device.

```python
import jax
import jax.numpy as jnp
from jax import lax

D = 6144
EXPERTS = 8
HID = 256
R_DEV = 16
CAP = 4
FFW = 8192
LAYERS = 8
MICRO = 8
ROWS = 512
SLOTS = 128
N_ET = 32


def draw_expert_ids(key, part):
    key = jax.random.fold_in(key, 11)
    keys = jax.random.split(key, 6)
    shape = (LAYERS, MICRO, N_ET)
    counts = jax.random.randint(keys[0], shape, 1, CAP + 1)
    full_batch = jax.random.randint(keys[1], (LAYERS,), 0, MICRO)
    batch_iota = jnp.arange(MICRO, dtype=jnp.int32)
    counts = jnp.where(batch_iota[None, :, None] == full_batch[:, None, None], CAP, counts)
    row_shape = (LAYERS, MICRO, N_ET, R_DEV)
    scores = jax.random.randint(keys[2], row_shape, 0, 1 << 20) * R_DEV + jnp.arange(R_DEV, dtype=jnp.int32)
    ranks = jnp.argsort(jnp.argsort(scores, axis=-1, stable=True), axis=-1, stable=True)
    chosen = ranks < counts[..., None]
    other = jax.random.randint(keys[3], row_shape, 1, EXPERTS)
    offset = jax.random.randint(keys[4], row_shape, 1, EXPERTS - 1)
    second = 1 + (other - 1 + offset) % (EXPERTS - 1)
    coin = jax.random.randint(keys[5], row_shape, 0, 2)
    first_id = jnp.where(chosen, jnp.where(coin == 1, 0, other), other)
    second_id = jnp.where(chosen, jnp.where(coin == 1, other, 0), second)
    both = jnp.stack([first_id, second_id], axis=-1)
    return both.reshape(LAYERS, MICRO, N_ET * R_DEV, 2).astype(jnp.int32)


def block_levels(key, extent, shards, least, top_value):
    level = 1.0
    for axis_at, parts in shards:
        draws = jax.random.uniform(jax.random.fold_in(jax.random.fold_in(key, 6), axis_at), (parts,), jnp.float32, least / len(shards), top_value / len(shards))
        level = level * jnp.repeat(jnp.exp(draws), extent[axis_at] // parts).reshape((-1,) + (1,) * (len(extent) - 1 - axis_at))
    return level


def gaussian(key, dims, width, limit, cuts=(), kind=jnp.bfloat16):
    level = block_levels(key, dims, cuts, -0.22, 0.18) if cuts else 1.0
    array = jax.random.normal(key, dims, jnp.float32) * width * level
    return jnp.minimum(jnp.maximum(array, -limit), limit).astype(kind)


def setup_inputs(seed: int = 0) -> dict:
    key_list = jax.random.split(jax.random.key(seed), 8)
    acts = gaussian(key_list[0], (MICRO, ROWS, D), 1.0, 6.0, ((0, 8), (1, 32)))
    norm_gain = jnp.clip(0.5 + 1.0 * jax.random.uniform(key_list[1], (LAYERS, D), jnp.float32) ** block_levels(key_list[1], (LAYERS, D), ((0, 8),), -0.2, 0.2), 0.5, 1.5)
    router = gaussian(key_list[2], (LAYERS, D, EXPERTS), D ** -0.5, 0.078125, ((0, 8),))
    w_gate = gaussian(key_list[3], (LAYERS, D, FFW), D ** -0.5, 0.078125, ((0, 8), (2, 32)))
    w_up = gaussian(key_list[4], (LAYERS, D, FFW), D ** -0.5, 0.078125, ((0, 8), (2, 32)))
    w_down = gaussian(key_list[5], (LAYERS, FFW, D), FFW ** -0.5, 0.0625, ((0, 8), (1, 32)))
    expert_ids = draw_expert_ids(jax.random.fold_in(key_list[7], 71), 0)
    return dict(acts=acts, norm_gain=norm_gain, router=router, w_gate=w_gate, w_up=w_up, w_down=w_down, expert_ids=expert_ids)


def expert_layer(current, gain, router, w_gate, w_up, w_down, routing):
    xf = current.astype(jnp.float32)
    scale = lax.rsqrt(lax.optimization_barrier(jnp.mean(xf * xf, axis=-1, keepdims=True)) + 1e-05)
    normed = (xf * scale * gain).astype(jnp.bfloat16)
    logits = jnp.dot(normed, router, preferred_element_type=jnp.float32)
    columns = jnp.arange(EXPERTS, dtype=jnp.int32)
    first = routing[:, 0]
    second = routing[:, 1]
    l_first = lax.optimization_barrier(jnp.sum(jnp.where(columns[None, :] == first[:, None], logits, 0.0), axis=-1))
    l_second = lax.optimization_barrier(jnp.sum(jnp.where(columns[None, :] == second[:, None], logits, 0.0), axis=-1))
    held = (first == 0) | (second == 0)
    rival = jnp.where(first == 0, l_second, l_first)
    gate = jnp.where(held, jax.nn.sigmoid(logits[:, 0] - rival), jnp.float32(0.0))
    held_rows = held.reshape(N_ET, R_DEV)
    position = jnp.cumsum(held_rows.astype(jnp.int32), axis=1) - 1
    slot_ids = jnp.arange(CAP, dtype=jnp.int32)
    select = (held_rows[:, None, :] & (position[:, None, :] == slot_ids[None, :, None])).astype(jnp.float32)
    slots = jnp.einsum('jcr,jrd->jcd', select, normed.astype(jnp.float32).reshape(N_ET, R_DEV, D), precision=lax.Precision.HIGHEST).astype(jnp.bfloat16).reshape(SLOTS, D)
    hidden = (jax.nn.silu(jnp.dot(slots, w_gate, preferred_element_type=jnp.float32)) * jnp.dot(slots, w_up, preferred_element_type=jnp.float32)).astype(jnp.bfloat16)
    terms = jnp.einsum('snh,nhd->nsd', hidden.astype(jnp.float32).reshape(SLOTS, N_ET, HID), w_down.astype(jnp.float32).reshape(N_ET, HID, D), precision=lax.Precision.HIGHEST)
    rounded = lax.optimization_barrier(terms.astype(jnp.bfloat16)).astype(jnp.float32)
    expert_out = lax.optimization_barrier(jnp.sum(rounded, axis=0))
    back = jnp.einsum('jcr,jcd->jrd', select, expert_out.reshape(N_ET, CAP, D), precision=lax.Precision.HIGHEST).reshape(ROWS, D)
    return (xf + gate[:, None] * back).astype(jnp.bfloat16)

def reference(acts, norm_gain, router, w_gate, w_up, w_down, expert_ids):
    results = []
    for batch_no in range(MICRO):
        current = acts[batch_no]
        for layer_no in range(batch_no, LAYERS):
            current = expert_layer(current, norm_gain[layer_no], router[layer_no], w_gate[layer_no], w_up[layer_no], w_down[layer_no], expert_ids[layer_no, batch_no])
        results.append(current)
    return jnp.stack(results)
```

```python
import functools
import math

import jax
import jax.numpy as jnp
from jax import lax
from jax.experimental import pallas as pl
from jax.experimental.pallas import tpu as pltpu
from jax.sharding import PartitionSpec as P

MESH = pl.DeviceIdType.MESH
F32 = jnp.float32
BF16 = jnp.bfloat16
CAP = 4
FOLD = 4
EPS = 1e-05


def iota(shape, dim):
    return lax.broadcasted_iota(jnp.int32, shape, dim)


def contract(a, b, dim_a, dim_b):
    return lax.dot_general(a, b, (((dim_a,), (dim_b,)), ((), ())), preferred_element_type=F32)


def relay_kernel(
    sections, side, acts, gain, router, w_gate, w_up, w_down, ids, out,
    wg, wu, wd, gathered, terms, landed, rows, chosen, early_out, early_in, late_out, late_in,
    xg, spread, perm, grow, gain_fold, next_route, next_pre, gates,
    w_local, w_send, w_recv, ag_send, ag_recv, rs_send, rs_recv, z_send, z_recv, credit,
):
    chips = side * side
    n_rows, depth = acts.shape[1], acts.shape[2]
    width = depth // FOLD
    hid = w_down.shape[1]
    lanes = FOLD * n_rows
    block = FOLD * CAP
    total = chips * block
    taken = chips * CAP

    section = lax.axis_index("section")
    et = lax.axis_index("et")
    core = lax.rem(et, 2)
    chip = et // 2
    cx = chip // side
    cy = lax.rem(chip, side)

    offsets = [(dx, dy) for dx in range(side) for dy in range(side) if dx or dy]
    offsets.sort(key=lambda o: -(min(o[0], side - o[0]) + min(o[1], side - o[1])))
    peers = []
    for dx, dy in offsets:
        there = lax.rem(cx + dx, side) * side + lax.rem(cy + dy, side)
        peers.append((there, (section, there * 2 + core)))
    sibling = (section, chip * 2 + 1 - core)
    above = (lax.rem(section + 1, sections), et)
    below = (lax.rem(section + sections - 1, sections), et)

    barrier = pltpu.get_barrier_semaphore()
    partners = [d for _, d in peers] + [sibling, above, below]
    for device in partners:
        pl.semaphore_signal(barrier, inc=1, device_id=device, device_id_type=MESH)

    loads = [
        pltpu.make_async_copy(src.at[0], dst.at[0], w_local.at[i])
        for i, (src, dst) in enumerate(((w_gate, wg), (w_up, wu), (w_down, wd)))
    ]
    for load in loads:
        load.start()

    def routing(turn):
        batch = lax.rem(section - turn + 2 * sections, sections)
        both = ids[0, batch].astype(F32)
        first, second = both[:, 0:1], both[:, 1:2]
        held = jnp.where((first == 0.0) | (second == 0.0), 1.0, 0.0) * (turn <= section).astype(F32)
        other = (first + second) * held
        row = iota((n_rows, lanes), 0)
        lane_row = lax.rem(iota((n_rows, lanes), 1), n_rows)
        same = row == lane_row
        held_lane = jnp.sum(jnp.where(same, held, 0.0), axis=0, keepdims=True)
        other_lane = jnp.sum(jnp.where(same, other, 0.0), axis=0, keepdims=True)
        place = jnp.sum(jnp.where(row <= lane_row, held, 0.0), axis=0, keepdims=True) - 1.0
        i = iota((block, lanes), 0)
        j = iota((block, lanes), 1)
        match = (i // CAP == j // n_rows) & (lax.rem(i, CAP).astype(F32) == place) & (held_lane > 0.0)
        select = jnp.where(match, 1.0, 0.0)
        rival = jnp.sum(select * other_lane, axis=1, keepdims=True)
        valid = jnp.sum(select, axis=1, keepdims=True)
        diag = iota((lanes, lanes), 0) == iota((lanes, lanes), 1)
        keep = jnp.where(diag & (held_lane == 0.0), 1.0, 0.0).astype(BF16)
        return select.astype(BF16), rival, valid, keep

    i = iota((total, total), 0)
    j = iota((total, total), 1)
    source = lax.rem(i, taken) // CAP * block + i // taken * CAP + lax.rem(i, CAP)
    perm[...] = jnp.where(j == source, 1.0, 0.0).astype(BF16)
    i = iota((total, taken), 0)
    j = iota((total, taken), 1)
    grow[...] = jnp.where(j == i // block * CAP + lax.rem(i, CAP), 1.0, 0.0).astype(BF16)
    fold_of = iota((block, 1), 0) // CAP
    folded = jnp.zeros((block, width), F32)
    for a in range(FOLD):
        folded = jnp.where(fold_of == a, gain[0:1, a * width : (a + 1) * width], folded)
    gain_fold[...] = folded

    for a in range(FOLD):
        rows[a * n_rows : (a + 1) * n_rows, :] = acts[0, :, a * width : (a + 1) * width]
    select, _, _, _ = routing(0)
    chosen[...] = jnp.dot(select, rows[...], preferred_element_type=F32).astype(BF16)
    gathered[chip] = chosen[...]

    pl.semaphore_wait(barrier, len(partners))

    gather = [
        pltpu.make_async_remote_copy(
            src_ref=chosen, dst_ref=gathered.at[chip], send_sem=ag_send.at[n], recv_sem=ag_recv.at[n],
            device_id=device, device_id_type=MESH,
        )
        for n, (_, device) in enumerate(peers)
    ]
    scatter = [
        pltpu.make_async_remote_copy(
            src_ref=terms.at[there], dst_ref=landed.at[chip], send_sem=rs_send.at[n], recv_sem=rs_recv.at[n],
            device_id=device, device_id_type=MESH,
        )
        for n, (there, device) in enumerate(peers)
    ]
    early = pltpu.make_async_remote_copy(
        src_ref=early_out, dst_ref=early_in, send_sem=z_send.at[0], recv_sem=z_recv.at[0],
        device_id=above, device_id_type=MESH,
    )
    late = pltpu.make_async_remote_copy(
        src_ref=late_out, dst_ref=late_in, send_sem=z_send.at[1], recv_sem=z_recv.at[1],
        device_id=above, device_id_type=MESH,
    )
    for copy in gather:
        copy.start()
    swaps = [
        pltpu.make_async_remote_copy(
            src_ref=src.at[0], dst_ref=dst.at[1], send_sem=w_send.at[i], recv_sem=w_recv.at[i],
            device_id=sibling, device_id_type=MESH,
        )
        for i, (src, dst) in enumerate(((w_gate, wg), (w_up, wu), (w_down, wd)))
    ]
    for swap in swaps:
        swap.start()

    def merged():
        incoming = contract(early_in[lanes : lanes + block, 0:lanes], late_in[...], 0, 0)
        return (early_in[0:lanes, :].astype(F32) + incoming).astype(BF16)

    def turn_body(turn, carry):
        @pl.when(turn > 0)
        def _():
            rows[...] = merged()
            pl.semaphore_signal(credit, inc=1, device_id=below, device_id_type=MESH)

        select, rival, valid, keep = routing(turn)

        @pl.when(turn > 0)
        def _():
            early.wait_send()
            late.wait_send()

        early_out[0:lanes, :] = jnp.dot(keep, rows[...], preferred_element_type=F32).astype(BF16)
        early_out[lanes : lanes + block, 0:lanes] = select

        @pl.when(turn > 0)
        def _():
            pl.semaphore_wait(credit, 1)

        early.start()

        x = chosen[...].astype(F32)
        weighted = (x * gain_fold[...]).astype(BF16)
        partial = jnp.zeros((block, router.shape[2]), F32)
        for a in range(FOLD):
            part = jnp.dot(weighted, router[0, a * width : (a + 1) * width, :], preferred_element_type=F32)
            partial = jnp.where(fold_of == a, part, partial)
        square = jnp.sum(x * x, axis=1, keepdims=True)
        logits = jnp.zeros_like(partial)
        squares = jnp.zeros_like(square)
        row_slot = lax.rem(iota((block, 1), 0), CAP)
        for slot in range(CAP):
            here = row_slot == slot
            logits = jnp.where(here, jnp.sum(jnp.where(here, partial, 0.0), axis=0, keepdims=True), logits)
            squares = jnp.where(here, jnp.sum(jnp.where(here, square, 0.0), axis=0, keepdims=True), squares)
        logits = logits * lax.rsqrt(squares / depth + EPS)
        expert = iota(logits.shape, 1).astype(F32)
        l_rival = jnp.sum(jnp.where(expert == rival, logits, 0.0), axis=1, keepdims=True)
        gates[...] = jnp.broadcast_to(valid * jax.nn.sigmoid(logits[:, 0:1] - l_rival), gates.shape)

        for copy in reversed(gather):
            copy.wait_recv()
        everyone = gathered[...].reshape(total, width)
        ordered = jnp.dot(perm[...], everyone, preferred_element_type=F32)
        square = jnp.zeros((taken, 1), F32)
        for a in range(FOLD):
            piece = ordered[a * taken : (a + 1) * taken, :]
            square = square + jnp.sum(piece * piece, axis=1, keepdims=True)
            xg[:, a * width : (a + 1) * width] = (piece * gain[0:1, a * width : (a + 1) * width]).astype(BF16)
        scale = lax.rsqrt(square / depth + EPS)

        @pl.when(turn == 0)
        def _():
            for copy in loads[:2]:
                copy.wait()
            for copy in swaps[:2]:
                copy.wait()

        hidden = []
        for half in range(2):
            g = jnp.dot(xg[...], wg[half], preferred_element_type=F32) * scale
            u = jnp.dot(xg[...], wu[half], preferred_element_type=F32) * scale
            hidden.append((jax.nn.silu(g) * u).astype(BF16))
        row_fold = lax.rem(iota((total, hid), 0), block) // CAP
        for half in range(2):
            wide = jnp.dot(grow[...], hidden[half], preferred_element_type=F32)
            for a in range(FOLD):
                spread[:, (a * 2 + half) * hid : (a * 2 + half + 1) * hid] = jnp.where(
                    row_fold == a, wide, 0.0
                ).astype(BF16)

        @pl.when(turn == 0)
        def _():
            loads[2].wait()
            swaps[2].wait()

        step = math.gcd(width, 256)
        for n in range(0, width, step):
            acc = jnp.zeros((total, step), F32)
            for a in range(FOLD):
                for half in range(2):
                    acc = acc + jnp.dot(
                        spread[:, (a * 2 + half) * hid : (a * 2 + half + 1) * hid],
                        wd[half, :, a * width + n : a * width + n + step],
                        preferred_element_type=F32,
                    )
            terms[:, :, n : n + step] = acc.astype(BF16).reshape(chips, block, step)
        for copy in scatter:
            copy.start()

        landed[chip] = terms[chip]
        for copy in gather:
            copy.wait_send()
        early.wait_recv()
        ahead, _, _, _ = routing(turn + 1)
        next_pre[...] = jnp.dot(ahead, early_in[0:lanes, :], preferred_element_type=F32)
        next_route[...] = contract(ahead, early_in[lanes : lanes + block, 0:lanes], 1, 1).astype(BF16)

        for copy in reversed(scatter):
            copy.wait_recv()
        sums = landed[0].astype(F32)
        for source_chip in range(1, chips):
            sums = sums + landed[source_chip].astype(F32)
        late_out[...] = (chosen[...].astype(F32) + gates[:, 0:1] * sums).astype(BF16)
        late.start()
        for copy in scatter:
            copy.wait_send()
        late.wait_recv()
        picked = next_pre[...] + jnp.dot(next_route[...], late_in[...], preferred_element_type=F32)

        @pl.when(turn < sections - 1)
        def _():
            chosen[...] = picked.astype(BF16)
            for copy in gather:
                copy.start()
            gathered[chip] = chosen[...]

        return carry

    lax.fori_loop(0, sections, turn_body, 0)

    final = merged()
    for a in range(FOLD):
        out[0, :, a * width : (a + 1) * width] = final[a * n_rows : (a + 1) * n_rows, :]
    early.wait_send()
    late.wait_send()


def body(sections, side, acts, norm_gain, router, w_gate, w_up, w_down, expert_ids):
    chips = side * side
    n_rows, depth = acts.shape[1], acts.shape[2]
    width = depth // FOLD
    hid = w_gate.shape[2]
    lanes = FOLD * n_rows
    block = FOLD * CAP
    total = chips * block
    taken = chips * CAP
    peers = chips - 1
    vmem = pl.BlockSpec(memory_space=pltpu.VMEM)
    hbm = pl.BlockSpec(memory_space=pl.ANY)
    dma = pltpu.SemaphoreType.DMA
    return pl.pallas_call(
        functools.partial(relay_kernel, sections, side),
        out_shape=jax.ShapeDtypeStruct(acts.shape, acts.dtype),
        in_specs=[vmem, vmem, vmem, hbm, hbm, hbm, vmem],
        out_specs=vmem,
        scratch_shapes=[
            pltpu.VMEM((2, depth, hid), BF16),
            pltpu.VMEM((2, depth, hid), BF16),
            pltpu.VMEM((2, hid, depth), BF16),
            pltpu.VMEM((chips, block, width), BF16),
            pltpu.VMEM((chips, block, width), BF16),
            pltpu.VMEM((chips, block, width), BF16),
            pltpu.VMEM((lanes, width), BF16),
            pltpu.VMEM((block, width), BF16),
            pltpu.VMEM((lanes + block, width), BF16),
            pltpu.VMEM((lanes + block, width), BF16),
            pltpu.VMEM((block, width), BF16),
            pltpu.VMEM((block, width), BF16),
            pltpu.VMEM((taken, depth), BF16),
            pltpu.VMEM((total, 2 * FOLD * hid), BF16),
            pltpu.VMEM((total, total), BF16),
            pltpu.VMEM((total, taken), BF16),
            pltpu.VMEM((block, width), F32),
            pltpu.VMEM((block, block), BF16),
            pltpu.VMEM((block, width), F32),
            pltpu.VMEM((block, 128), F32),
            dma((3,)), dma((3,)), dma((3,)),
            dma((peers,)), dma((peers,)), dma((peers,)), dma((peers,)),
            dma((2,)), dma((2,)),
            pltpu.SemaphoreType.REGULAR,
        ],
        compiler_params=pltpu.CompilerParams(
            collective_id=0, has_side_effects=True, vmem_limit_bytes=48 * 2**20
        ),
        name="relay",
    )(acts, norm_gain, router, w_gate, w_up, w_down, expert_ids)


def solution(mesh):
    sections, et = mesh.shape["section"], mesh.shape["et"]
    side = math.isqrt(et // 2)
    return jax.shard_map(
        functools.partial(body, sections, side),
        mesh=mesh,
        in_specs=(
            P("section", "et", None),
            P("section", None),
            P("section", None, None),
            P("section", None, "et"),
            P("section", None, "et"),
            P("section", "et", None),
            P("section", None, "et", None),
        ),
        out_specs=P("section", "et", None),
        check_vma=False,
    )
```

```python
import functools
import math

import jax
import jax.numpy as jnp
from jax import lax
from jax.experimental import pallas as pl
from jax.experimental.pallas import tpu as pltpu
from jax.sharding import PartitionSpec as P

MESH = pl.DeviceIdType.MESH
F32 = jnp.float32
BF16 = jnp.bfloat16
CAP = 4
FOLD = 4
PATHS = 2
EPS = 1e-05


def iota(shape, dim):
    return lax.broadcasted_iota(jnp.int32, shape, dim)


def contract(a, b, dim_a, dim_b):
    return lax.dot_general(a, b, (((dim_a,), (dim_b,)), ((), ())), preferred_element_type=F32)


def far_first(side):
    return sorted(range(1, side), key=lambda d: (-min(d, side - d), d))


def relay_kernel(
    sections, side, acts_hbm, gain_hbm, router_hbm, w_gate, w_up, w_down, ids_hbm, out,
    acts, gain, router, ids,
    wg, wu, wd, gathered, terms, mid, mid_sum, landed, rows, chosen, early_out, early_in, late_out, late_in,
    xg, sums_gu, spread, perm, grow, gain_fold, next_route, next_pre, gates,
    in_sem, w_local, w_send, w_recv, ag1_send, ag1_recv, ag2_send, ag2_recv,
    rs1_send, rs1_recv, rs2_send, rs2_recv, z_send, z_recv, credit,
):
    chips = side * side
    n_rows, depth = acts.shape[1], acts.shape[2]
    part = depth // PATHS
    width = part // FOLD
    hid = w_down.shape[1]
    lanes = FOLD * n_rows
    block = FOLD * CAP
    total = chips * block
    taken = chips * CAP

    section = lax.axis_index("section")
    et = lax.axis_index("et")
    core = lax.rem(et, 2)
    chip = et // 2
    cx = chip // side
    cy = lax.rem(chip, side)

    def chip_at(dx, dy):
        return lax.rem(cx + dx, side) * side + lax.rem(cy + dy, side)

    def device_at(dx, dy):
        return (section, chip_at(dx, dy) * 2 + core)

    def along(axis, d):
        return (d, 0) if axis == 0 else (0, d)

    def place(axis):
        return cx if axis == 0 else cy

    order = far_first(side)
    sibling = (section, chip * 2 + 1 - core)
    above = (lax.rem(section + 1, sections), et)
    below = (lax.rem(section + sections - 1, sections), et)

    barrier = pltpu.get_barrier_semaphore()
    partners = [device_at(*along(axis, d)) for axis in range(2) for d in order] + [sibling, above, below]
    for device in partners:
        pl.semaphore_signal(barrier, inc=1, device_id=device, device_id_type=MESH)

    inputs = [
        pltpu.make_async_copy(src, dst, in_sem.at[i])
        for i, (src, dst) in enumerate(
            ((acts_hbm, acts), (ids_hbm, ids), (gain_hbm, gain), (router_hbm, router))
        )
    ]
    for copy in inputs:
        copy.start()
    pieces = []
    for p in range(PATHS):
        for src, dst in ((w_gate, wg), (w_up, wu)):
            span = pl.ds(p * part, part)
            pieces.append((src.at[0, span], dst.at[0, span], dst.at[1, span]))
    pieces.append((w_down.at[0], wd.at[0], wd.at[1]))
    loads = [pltpu.make_async_copy(src, dst, w_local.at[i]) for i, (src, dst, _) in enumerate(pieces)]
    for load in loads:
        load.start()

    def routing(turn):
        batch = lax.rem(section - turn + 2 * sections, sections)
        both = ids[0, batch].astype(F32).astype(BF16)
        tile = jnp.where(iota((n_rows, lanes), 0) == lax.rem(iota((n_rows, lanes), 1), n_rows), 1.0, 0.0)
        lane_ids = jnp.dot(both, tile.astype(BF16), preferred_element_type=F32)
        first, second = lane_ids[0:1, :], lane_ids[1:2, :]
        held = jnp.where((first == 0.0) | (second == 0.0), 1.0, 0.0) * (turn <= section).astype(F32)
        other = (first + second) * held
        i = iota((lanes, lanes), 0)
        j = iota((lanes, lanes), 1)
        upto = jnp.where((i // n_rows == j // n_rows) & (i <= j), 1.0, 0.0).astype(BF16)
        spots = jnp.dot(jnp.broadcast_to(held, (8, lanes)).astype(BF16), upto, preferred_element_type=F32)
        spot = spots[0:1, :] - 1.0
        keep = jnp.where((i == j) & (held == 0.0), 1.0, 0.0).astype(BF16)
        i = iota((block, lanes), 0)
        j = iota((block, lanes), 1)
        match = (i // CAP == j // n_rows) & (lax.rem(i, CAP).astype(F32) == spot) & (held > 0.0)
        select = jnp.where(match, 1.0, 0.0)
        rival = jnp.sum(select * other, axis=1, keepdims=True)
        valid = jnp.sum(select, axis=1, keepdims=True)
        return select.astype(BF16), rival, valid, keep

    i = iota((total, total), 0)
    j = iota((total, total), 1)
    source = lax.rem(i, taken) // CAP * block + i // taken * CAP + lax.rem(i, CAP)
    perm[...] = jnp.where(j == source, 1.0, 0.0).astype(BF16)
    i = iota((total, taken), 0)
    j = iota((total, taken), 1)
    grow[...] = jnp.where(j == i // block * CAP + lax.rem(i, CAP), 1.0, 0.0).astype(BF16)
    fold_of = iota((block, 1), 0) // CAP

    def columns(p, a):
        return slice(p * part + a * width, p * part + (a + 1) * width)

    inputs[0].wait()
    inputs[1].wait()
    select, _, _, _ = routing(0)
    for p in range(PATHS):
        for a in range(FOLD):
            rows[p, a * n_rows : (a + 1) * n_rows, :] = acts[0, :, columns(p, a)]
        chosen[p] = jnp.dot(select, rows[p], preferred_element_type=F32).astype(BF16)

    pl.semaphore_wait(barrier, len(partners))

    def remote(src, dst, send, recv, device):
        return pltpu.make_async_remote_copy(
            src_ref=src, dst_ref=dst, send_sem=send, recv_sem=recv, device_id=device, device_id_type=MESH
        )

    def own_chip(p, d):
        dx, dy = along(p, side - d)
        return chip_at(dx, dy) if d else chip

    gather1 = [
        {
            d: remote(
                chosen.at[p], gathered.at[p, chip], ag1_send.at[p, d - 1], ag1_recv.at[p, d - 1],
                device_at(*along(p, d)),
            )
            for d in order
        }
        for p in range(PATHS)
    ]
    gather2 = [
        {
            (d, e): remote(
                chosen.at[p] if d == 0 else gathered.at[p, own_chip(p, d)],
                gathered.at[p, own_chip(p, d)],
                ag2_send.at[p, d, e - 1], ag2_recv.at[p, d, e - 1],
                device_at(*along(1 - p, e)),
            )
            for d in range(side)
            for e in order
        }
        for p in range(PATHS)
    ]
    scatter1 = [
        {
            (d, e): remote(
                terms.at[p, chip_at(*(d, e) if p == 0 else (e, d))],
                mid.at[p, side - e, d],
                rs1_send.at[p, d, e - 1], rs1_recv.at[p, d, e - 1],
                device_at(*along(1 - p, e)),
            )
            for d in range(side)
            for e in order
        }
        for p in range(PATHS)
    ]
    scatter2 = [
        {
            d: remote(
                mid_sum.at[p, d], landed.at[p, side - d], rs2_send.at[p, d - 1], rs2_recv.at[p, d - 1],
                device_at(*along(p, d)),
            )
            for d in order
        }
        for p in range(PATHS)
    ]
    early = remote(early_out, early_in, z_send.at[PATHS], z_recv.at[PATHS], above)
    late = [remote(late_out.at[p], late_in.at[p], z_send.at[p], z_recv.at[p], above) for p in range(PATHS)]
    swaps = [remote(src, dst, w_send.at[i], w_recv.at[i], sibling) for i, (src, _, dst) in enumerate(pieces)]

    def start_gather(p):
        for d in order:
            gather1[p][d].start()
        for e in order:
            gather2[p][0, e].start()
        gathered[p, chip] = chosen[p]

    def merged(p):
        incoming = contract(early_in[PATHS * lanes :, 0:lanes], late_in[p], 0, 0)
        return (early_in[p * lanes : (p + 1) * lanes, :].astype(F32) + incoming).astype(BF16)

    for p in range(PATHS):
        start_gather(p)
    for swap in swaps:
        swap.start()

    inputs[2].wait()
    inputs[3].wait()
    for p in range(PATHS):
        folded = jnp.zeros((block, width), F32)
        for a in range(FOLD):
            folded = jnp.where(fold_of == a, gain[0:1, columns(p, a)], folded)
        gain_fold[p] = folded

    def turn_body(turn, carry):
        for d in reversed(order):
            for p in range(PATHS):
                gather1[p][d].wait_recv()
                for e in order:
                    gather2[p][d, e].start()

        @pl.when(turn > 0)
        def _():
            for p in range(PATHS):
                rows[p] = merged(p)
            pl.semaphore_signal(credit, inc=1, device_id=below, device_id_type=MESH)

        select, rival, valid, keep = routing(turn)

        @pl.when(turn > 0)
        def _():
            early.wait_send()

        for p in range(PATHS):
            early_out[p * lanes : (p + 1) * lanes, :] = jnp.dot(
                keep, rows[p], preferred_element_type=F32
            ).astype(BF16)
        early_out[PATHS * lanes :, 0:lanes] = select

        @pl.when(turn > 0)
        def _():
            pl.semaphore_wait(credit, 1)

        early.start()

        partial = jnp.zeros((block, router.shape[1]), F32)
        square = jnp.zeros((block, 1), F32)
        for p in range(PATHS):
            x = chosen[p].astype(F32)
            weighted = (x * gain_fold[p]).astype(BF16)
            square = square + jnp.sum(x * x, axis=1, keepdims=True)
            for a in range(FOLD):
                piece = contract(weighted, router[0, :, columns(p, a)], 1, 1)
                partial = partial + jnp.where(fold_of == a, piece, 0.0)
        logits = jnp.zeros_like(partial)
        squares = jnp.zeros_like(square)
        row_slot = lax.rem(iota((block, 1), 0), CAP)
        for slot in range(CAP):
            here = row_slot == slot
            logits = jnp.where(here, jnp.sum(jnp.where(here, partial, 0.0), axis=0, keepdims=True), logits)
            squares = jnp.where(here, jnp.sum(jnp.where(here, square, 0.0), axis=0, keepdims=True), squares)
        logits = logits * lax.rsqrt(squares / depth + EPS)
        expert = iota(logits.shape, 1).astype(F32)
        l_rival = jnp.sum(jnp.where(expert == rival, logits, 0.0), axis=1, keepdims=True)
        gates[...] = jnp.broadcast_to(valid * jax.nn.sigmoid(logits[:, 0:1] - l_rival), gates.shape)

        square = jnp.zeros((taken, 1), F32)
        for p in range(PATHS):
            for d in (0, *reversed(order)):
                for e in reversed(order):
                    gather2[p][d, e].wait_recv()
            everyone = gathered[p].reshape(total, width)
            ordered = jnp.dot(perm[...], everyone, preferred_element_type=F32)
            for a in range(FOLD):
                piece = ordered[a * taken : (a + 1) * taken, :]
                square = square + jnp.sum(piece * piece, axis=1, keepdims=True)
                xg[:, a * width : (a + 1) * width] = (piece * gain[0:1, columns(p, a)]).astype(BF16)

            @pl.when(turn == 0)
            def _():
                for n in (2 * p, 2 * p + 1):
                    loads[n].wait()
                    swaps[n].wait()

            for half in range(2):
                for n, w in ((0, wg), (1, wu)):
                    dot = jnp.dot(xg[...], w[half, p * part : (p + 1) * part, :], preferred_element_type=F32)
                    span = slice((2 * n + half) * hid, (2 * n + half + 1) * hid)
                    if p == 0:
                        sums_gu[:, span] = dot
                    else:
                        sums_gu[:, span] = sums_gu[:, span] + dot
        scale = lax.rsqrt(square / depth + EPS)
        row_fold = lax.rem(iota((total, hid), 0), block) // CAP
        for half in range(2):
            g = sums_gu[:, half * hid : (half + 1) * hid] * scale
            u = sums_gu[:, (2 + half) * hid : (3 + half) * hid] * scale
            wide = jnp.dot(grow[...], (jax.nn.silu(g) * u).astype(BF16), preferred_element_type=F32)
            for a in range(FOLD):
                spread[:, (a * 2 + half) * hid : (a * 2 + half + 1) * hid] = jnp.where(
                    row_fold == a, wide, 0.0
                ).astype(BF16)

        @pl.when(turn == 0)
        def _():
            loads[4].wait()
            swaps[4].wait()

        step = math.gcd(width, 256)
        for p in range(PATHS):
            for n in range(0, width, step):
                acc = jnp.zeros((total, step), F32)
                for a in range(FOLD):
                    begin = p * part + a * width + n
                    for half in range(2):
                        acc = acc + jnp.dot(
                            spread[:, (a * 2 + half) * hid : (a * 2 + half + 1) * hid],
                            wd[half, :, begin : begin + step],
                            preferred_element_type=F32,
                        )
                terms[p, :, :, n : n + step] = acc.astype(BF16).reshape(chips, block, step)
            if p == PATHS - 1:
                for q in range(PATHS):
                    for copy in (*gather1[q].values(), *gather2[q].values()):
                        copy.wait_send()
            for d in (*order, 0):
                for e in order:
                    scatter1[p][d, e].start()

        for d in (*order, 0):
            for p in range(PATHS):
                here = chip_at(*along(p, d))
                value = terms[p, here].astype(F32)
                for e in reversed(order):
                    scatter1[p][d, e].wait_recv()
                    value = value + mid[p, side - e, d].astype(F32)
                if d:
                    mid_sum[p, d] = value.astype(BF16)
                    scatter2[p][d].start()
                else:
                    landed[p, 0] = value.astype(BF16)

        early.wait_recv()
        ahead, _, _, _ = routing(turn + 1)
        next_route[...] = contract(ahead, early_in[PATHS * lanes :, 0:lanes], 1, 1).astype(BF16)
        for p in range(PATHS):
            next_pre[p] = jnp.dot(ahead, early_in[p * lanes : (p + 1) * lanes, :], preferred_element_type=F32)

        for p in range(PATHS):

            @pl.when(turn > 0)
            def _():
                late[p].wait_send()

            result = landed[p, 0].astype(F32)
            for d in reversed(order):
                scatter2[p][d].wait_recv()
                result = result + landed[p, side - d].astype(F32)
            late_out[p] = (chosen[p].astype(F32) + gates[:, 0:1] * result).astype(BF16)
            late[p].start()
        for p in range(PATHS):
            for copy in (*scatter1[p].values(), *scatter2[p].values()):
                copy.wait_send()
        for p in range(PATHS):
            late[p].wait_recv()
            picked = next_pre[p] + jnp.dot(next_route[...], late_in[p], preferred_element_type=F32)

            @pl.when(turn < sections - 1)
            def _():
                chosen[p] = picked.astype(BF16)
                start_gather(p)

        return carry

    lax.fori_loop(0, sections, turn_body, 0)

    for p in range(PATHS):
        final = merged(p)
        for a in range(FOLD):
            out[0, :, columns(p, a)] = final[a * n_rows : (a + 1) * n_rows, :]
    early.wait_send()
    for p in range(PATHS):
        late[p].wait_send()


def body(sections, side, acts, norm_gain, router, w_gate, w_up, w_down, expert_ids):
    chips = side * side
    n_rows, depth = acts.shape[1], acts.shape[2]
    part = depth // PATHS
    width = part // FOLD
    hid = w_gate.shape[2]
    lanes = FOLD * n_rows
    block = FOLD * CAP
    total = chips * block
    taken = chips * CAP
    router = jnp.transpose(router, (0, 2, 1))
    expert_ids = jnp.transpose(expert_ids, (0, 1, 3, 2))
    hbm = pl.BlockSpec(memory_space=pl.ANY)
    dma = pltpu.SemaphoreType.DMA
    return pl.pallas_call(
        functools.partial(relay_kernel, sections, side),
        out_shape=jax.ShapeDtypeStruct(acts.shape, acts.dtype),
        in_specs=[hbm] * 7,
        out_specs=pl.BlockSpec(memory_space=pltpu.VMEM),
        scratch_shapes=[
            pltpu.VMEM(acts.shape, BF16),
            pltpu.VMEM(norm_gain.shape, F32),
            pltpu.VMEM(router.shape, BF16),
            pltpu.VMEM(expert_ids.shape, jnp.int32),
            pltpu.VMEM((2, depth, hid), BF16),
            pltpu.VMEM((2, depth, hid), BF16),
            pltpu.VMEM((2, hid, depth), BF16),
            pltpu.VMEM((PATHS, chips, block, width), BF16),
            pltpu.VMEM((PATHS, chips, block, width), BF16),
            pltpu.VMEM((PATHS, side, side, block, width), BF16),
            pltpu.VMEM((PATHS, side, block, width), BF16),
            pltpu.VMEM((PATHS, side, block, width), BF16),
            pltpu.VMEM((PATHS, lanes, width), BF16),
            pltpu.VMEM((PATHS, block, width), BF16),
            pltpu.VMEM((PATHS * lanes + block, width), BF16),
            pltpu.VMEM((PATHS * lanes + block, width), BF16),
            pltpu.VMEM((PATHS, block, width), BF16),
            pltpu.VMEM((PATHS, block, width), BF16),
            pltpu.VMEM((taken, part), BF16),
            pltpu.VMEM((taken, 4 * hid), F32),
            pltpu.VMEM((total, 2 * FOLD * hid), BF16),
            pltpu.VMEM((total, total), BF16),
            pltpu.VMEM((total, taken), BF16),
            pltpu.VMEM((PATHS, block, width), F32),
            pltpu.VMEM((block, block), BF16),
            pltpu.VMEM((PATHS, block, width), F32),
            pltpu.VMEM((block, 128), F32),
            dma((4,)), dma((5,)), dma((5,)), dma((5,)),
            dma((PATHS, side - 1)), dma((PATHS, side - 1)),
            dma((PATHS, side, side - 1)), dma((PATHS, side, side - 1)),
            dma((PATHS, side, side - 1)), dma((PATHS, side, side - 1)),
            dma((PATHS, side - 1)), dma((PATHS, side - 1)),
            dma((PATHS + 1,)), dma((PATHS + 1,)),
            pltpu.SemaphoreType.REGULAR,
        ],
        compiler_params=pltpu.CompilerParams(
            collective_id=0, has_side_effects=True, vmem_limit_bytes=60 * 2**20
        ),
        name="relay",
    )(acts, norm_gain, router, w_gate, w_up, w_down, expert_ids)


def solution(mesh):
    sections, et = mesh.shape["section"], mesh.shape["et"]
    side = math.isqrt(et // 2)
    return jax.shard_map(
        functools.partial(body, sections, side),
        mesh=mesh,
        in_specs=(
            P("section", "et", None),
            P("section", None),
            P("section", None, None),
            P("section", None, "et"),
            P("section", None, "et"),
            P("section", "et", None),
            P("section", None, "et", None),
        ),
        out_specs=P("section", "et", None),
        check_vma=False,
    )
```

```python
import functools
import math

import jax
import jax.numpy as jnp
from jax import lax
from jax.experimental import pallas as pl
from jax.experimental.pallas import tpu as pltpu
from jax.sharding import PartitionSpec as P

MESH = pl.DeviceIdType.MESH
F32 = jnp.float32
BF16 = jnp.bfloat16
CAP = 4
FOLD = 4
PATHS = 2
EPS = 1e-05


def iota(shape, dim):
    return lax.broadcasted_iota(jnp.int32, shape, dim)


def contract(a, b, dim_a, dim_b):
    return lax.dot_general(a, b, (((dim_a,), (dim_b,)), ((), ())), preferred_element_type=F32)


def far_first(side):
    return sorted(range(1, side), key=lambda d: (-min(d, side - d), d))


def relay_kernel(
    sections, side, acts_hbm, gain_hbm, router_hbm, w_gate, w_up, w_down, ids_hbm, out,
    acts, gain, router, ids,
    wg, wu, wd, gathered, terms, mid, mid_sum, landed, rows, chosen, early_out, early_in, fresh,
    xg, sums_gu, hidden, stacked, perm, perm_back, gain_fold, next_route, next_pre, gates_out, gates_in,
    in_sem, w_local, w_send, w_recv, ag_send, ag1_recv, ag2_recv,
    rs1_send, rs1_recv, rs2_send, rs2_recv, z_send, z_recv, credit_early, credit_landed,
):
    chips = side * side
    n_rows, depth = acts.shape[1], acts.shape[2]
    part = depth // PATHS
    width = part // FOLD
    hid = w_down.shape[1]
    lanes = FOLD * n_rows
    block = FOLD * CAP
    total = chips * block
    taken = chips * CAP

    section = lax.axis_index("section")
    et = lax.axis_index("et")
    core = lax.rem(et, 2)
    chip = et // 2
    cx = chip // side
    cy = lax.rem(chip, side)

    def chip_at(dx, dy):
        return lax.rem(cx + dx, side) * side + lax.rem(cy + dy, side)

    def device_at(dx, dy):
        return (section, chip_at(dx, dy) * 2 + core)

    def along(axis, d):
        return (d, 0) if axis == 0 else (0, d)

    def place(axis):
        return cx if axis == 0 else cy

    order = far_first(side)
    sibling = (section, chip * 2 + 1 - core)
    next_section = lax.rem(section + 1, sections)
    last_section = lax.rem(section + sections - 1, sections)
    above = (next_section, chip * 2 + 1 - core)
    below = (last_section, chip * 2 + 1 - core)

    barrier = pltpu.get_barrier_semaphore()
    partners = [sibling, above, below]
    for axis in range(2):
        for d in order:
            there = chip_at(*along(axis, d)) * 2
            partners += [
                (section, there + core), (next_section, there + 1 - core), (last_section, there + 1 - core)
            ]
    for device in partners:
        pl.semaphore_signal(barrier, inc=1, device_id=device, device_id_type=MESH)

    inputs = [
        pltpu.make_async_copy(src, dst, in_sem.at[i])
        for i, (src, dst) in enumerate(
            ((acts_hbm, acts), (ids_hbm.at[0], ids.at[0]), (gain_hbm, gain), (router_hbm, router))
        )
    ]
    for copy in inputs:
        copy.start()
    pieces = []
    for p in range(PATHS):
        for src, dst in ((w_gate, wg), (w_up, wu)):
            span = pl.ds(p * part, part)
            pieces.append((src.at[0, span], dst.at[0, span], dst.at[1, span]))
    pieces.append((w_down.at[0], wd.at[pl.ds(0, hid)], wd.at[pl.ds(hid, hid)]))
    loads = [pltpu.make_async_copy(src, dst, w_local.at[i]) for i, (src, dst, _) in enumerate(pieces)]
    for load in loads:
        load.start()

    def routing(turn):
        batch = lax.rem(section - turn + 2 * sections, sections)
        both = ids[lax.rem(turn, 2), batch].astype(F32).astype(BF16)
        tile = jnp.where(iota((n_rows, lanes), 0) == lax.rem(iota((n_rows, lanes), 1), n_rows), 1.0, 0.0)
        lane_ids = jnp.dot(both, tile.astype(BF16), preferred_element_type=F32)
        first, second = lane_ids[0:1, :], lane_ids[1:2, :]
        held = jnp.where((first == 0.0) | (second == 0.0), 1.0, 0.0) * (turn <= section).astype(F32)
        other = (first + second) * held
        i = iota((lanes, lanes), 0)
        j = iota((lanes, lanes), 1)
        upto = jnp.where((i // n_rows == j // n_rows) & (i <= j), 1.0, 0.0).astype(BF16)
        spots = jnp.dot(jnp.broadcast_to(held, (8, lanes)).astype(BF16), upto, preferred_element_type=F32)
        spot = spots[0:1, :] - 1.0
        keep = jnp.where((i == j) & (held == 0.0), 1.0, 0.0).astype(BF16)
        i = iota((block, lanes), 0)
        j = iota((block, lanes), 1)
        match = (i // CAP == j // n_rows) & (lax.rem(i, CAP).astype(F32) == spot) & (held > 0.0)
        select = jnp.where(match, 1.0, 0.0)
        rival = jnp.sum(select * other, axis=1, keepdims=True)
        valid = jnp.sum(select, axis=1, keepdims=True)
        return select.astype(BF16), rival, valid, keep

    i = iota((total, total), 0)
    j = iota((total, total), 1)
    source = lax.rem(i, taken) // CAP * block + i // taken * CAP + lax.rem(i, CAP)
    perm[...] = jnp.where(j == source, 1.0, 0.0).astype(BF16)
    source = lax.rem(i, block) // CAP * taken + i // block * CAP + lax.rem(i, CAP)
    perm_back[...] = jnp.where(j == source, 1.0, 0.0).astype(BF16)
    fold_of = iota((block, 1), 0) // CAP

    def columns(p, a):
        return slice(p * part + a * width, p * part + (a + 1) * width)

    inputs[0].wait()
    inputs[1].wait()
    select, _, _, _ = routing(0)
    for p in range(PATHS):
        for a in range(FOLD):
            rows[p, a * n_rows : (a + 1) * n_rows, :] = acts[0, :, columns(p, a)]
        chosen[p] = jnp.dot(select, rows[p], preferred_element_type=F32).astype(BF16)

    pl.semaphore_wait(barrier, len(partners))

    def remote(src, dst, send, recv, device):
        return pltpu.make_async_remote_copy(
            src_ref=src, dst_ref=dst, send_sem=send, recv_sem=recv, device_id=device, device_id_type=MESH
        )

    def own_chip(p, d):
        dx, dy = along(p, side - d)
        return chip_at(dx, dy) if d else chip

    gather1 = [
        {
            d: remote(
                chosen.at[p], gathered.at[p, chip], ag_send.at[p], ag1_recv.at[p, d - 1],
                device_at(*along(p, d)),
            )
            for d in order
        }
        for p in range(PATHS)
    ]
    gather2 = [
        {
            (d, e): remote(
                chosen.at[p] if d == 0 else gathered.at[p, own_chip(p, d)],
                gathered.at[p, own_chip(p, d)],
                ag_send.at[p], ag2_recv.at[p],
                device_at(*along(1 - p, e)),
            )
            for d in range(side)
            for e in order
        }
        for p in range(PATHS)
    ]
    scatter1 = [
        {
            (d, e): remote(
                terms.at[p, chip_at(*(d, e) if p == 0 else (e, d))],
                mid.at[p, side - e, d],
                rs1_send.at[p], rs1_recv.at[p, d],
                device_at(*along(1 - p, e)),
            )
            for d in range(side)
            for e in order
        }
        for p in range(PATHS)
    ]
    scatter2 = [
        {
            d: remote(
                mid_sum.at[p, d], landed.at[p, (side - d) % side], rs2_send.at[p], rs2_recv.at[p],
                (next_section, chip_at(*along(p, d)) * 2 + 1 - core),
            )
            for d in range(side)
        }
        for p in range(PATHS)
    ]
    early = [
        remote(early_out, early_in, z_send.at[0], z_recv.at[0], above),
        remote(gates_out, gates_in, z_send.at[1], z_recv.at[1], above),
    ]
    swap_ids = remote(ids.at[0], ids.at[1], w_send.at[len(pieces)], w_recv.at[len(pieces)], sibling)
    few, many = side - 1, side * (side - 1)

    def sent(ref, sem):
        remote(ref, ref, sem, sem, sibling).wait_send()

    def came(ref, sem):
        remote(ref, ref, sem, sem, sibling).wait_recv()

    swaps = [remote(src, dst, w_send.at[i], w_recv.at[i], sibling) for i, (src, _, dst) in enumerate(pieces)]

    def start_gather(p):
        for d in order:
            gather1[p][d].start()
        for e in order:
            gather2[p][0, e].start()
        gathered[p, chip] = chosen[p]

    routes = slice(PATHS * lanes, PATHS * lanes + block)
    slots_at = [slice(routes.stop + p * block, routes.stop + (p + 1) * block) for p in range(PATHS)]

    def merged(p):
        incoming = contract(early_in[routes, 0:lanes], fresh[p], 0, 0)
        return (early_in[p * lanes : (p + 1) * lanes, :].astype(F32) + incoming).astype(BF16)

    for p in range(PATHS):
        start_gather(p)
    swap_ids.start()
    for swap in swaps:
        swap.start()

    inputs[2].wait()
    inputs[3].wait()
    for p in range(PATHS):
        folded = jnp.zeros((block, width), F32)
        for a in range(FOLD):
            folded = jnp.where(fold_of == a, gain[0:1, columns(p, a)], folded)
        gain_fold[p] = folded

    def turn_body(turn, carry):
        for p in range(PATHS):
            if p == PATHS - 1:

                @pl.when(turn > 0)
                def _():
                    pl.semaphore_wait(credit_landed, 1)

            for d in reversed(order):
                gather1[p][d].wait_recv()
                for e in order:
                    gather2[p][d, e].start()

        @pl.when(turn > 0)
        def _():
            for p in range(PATHS):
                rows[p] = merged(p)
            pl.semaphore_signal(credit_early, inc=1, device_id=below, device_id_type=MESH)

        select, rival, valid, keep = routing(turn)

        partial = jnp.zeros((block, router.shape[1]), F32)
        square = jnp.zeros((block, 1), F32)
        for p in range(PATHS):
            x = chosen[p].astype(F32)
            weighted = (x * gain_fold[p]).astype(BF16)
            square = square + jnp.sum(x * x, axis=1, keepdims=True)
            for a in range(FOLD):
                piece = contract(weighted, router[0, :, columns(p, a)], 1, 1)
                partial = partial + jnp.where(fold_of == a, piece, 0.0)
        logits = jnp.zeros_like(partial)
        squares = jnp.zeros_like(square)
        row_slot = lax.rem(iota((block, 1), 0), CAP)
        for slot in range(CAP):
            here = row_slot == slot
            logits = jnp.where(here, jnp.sum(jnp.where(here, partial, 0.0), axis=0, keepdims=True), logits)
            squares = jnp.where(here, jnp.sum(jnp.where(here, square, 0.0), axis=0, keepdims=True), squares)
        logits = logits * lax.rsqrt(squares / depth + EPS)
        expert = iota(logits.shape, 1).astype(F32)
        l_rival = jnp.sum(jnp.where(expert == rival, logits, 0.0), axis=1, keepdims=True)
        gate = valid * jax.nn.sigmoid(logits[:, 0:1] - l_rival)

        @pl.when(turn > 0)
        def _():
            for copy in early:
                copy.wait_send()

        for p in range(PATHS):
            early_out[p * lanes : (p + 1) * lanes, :] = jnp.dot(
                keep, rows[p], preferred_element_type=F32
            ).astype(BF16)
            early_out[slots_at[p], :] = chosen[p]
        early_out[routes, 0:lanes] = select
        gates_out[...] = jnp.broadcast_to(gate, gates_out.shape)

        @pl.when(turn > 0)
        def _():
            pl.semaphore_wait(credit_early, 1)

        for copy in early:
            copy.start()

        square = jnp.zeros((taken, 1), F32)
        for p in range(PATHS):
            came(gathered.at[p, pl.ds(0, many)], ag2_recv.at[p])
            everyone = gathered[p].reshape(total, width)
            ordered = jnp.dot(perm[...], everyone, preferred_element_type=F32)
            for a in range(FOLD):
                piece = ordered[a * taken : (a + 1) * taken, :]
                square = square + jnp.sum(piece * piece, axis=1, keepdims=True)
                xg[:, a * width : (a + 1) * width] = (piece * gain[0:1, columns(p, a)]).astype(BF16)

            @pl.when(turn == 0)
            def _():
                for n in (2 * p, 2 * p + 1):
                    loads[n].wait()
                    swaps[n].wait()

            for half in range(2):
                for n, w in ((0, wg), (1, wu)):
                    dot = jnp.dot(xg[...], w[half, p * part : (p + 1) * part, :], preferred_element_type=F32)
                    span = slice((2 * n + half) * hid, (2 * n + half + 1) * hid)
                    if p == 0:
                        sums_gu[:, span] = dot
                    else:
                        sums_gu[:, span] = sums_gu[:, span] + dot
        scale = lax.rsqrt(square / depth + EPS)
        for half in range(2):
            g = sums_gu[:, half * hid : (half + 1) * hid] * scale
            u = sums_gu[:, (2 + half) * hid : (3 + half) * hid] * scale
            hidden[:, half * hid : (half + 1) * hid] = (jax.nn.silu(g) * u).astype(BF16)

        @pl.when(turn == 0)
        def _():
            loads[4].wait()
            swaps[4].wait()

        for p in range(PATHS):
            for a in range(FOLD):
                stacked[a * taken : (a + 1) * taken, :] = jnp.dot(
                    hidden[...], wd[:, columns(p, a)], preferred_element_type=F32
                ).astype(BF16)
            reordered = jnp.dot(perm_back[...], stacked[...], preferred_element_type=F32)
            terms[p] = reordered.astype(BF16).reshape(chips, block, width)
            if p == 0:
                for q in range(PATHS):
                    sent(gathered.at[q, pl.ds(0, few + many)], ag_send.at[q])
            for d in (*order, 0):
                for e in order:
                    scatter1[p][d, e].start()

        for p in range(PATHS):
            for d in (*order, 0):
                here = chip_at(*along(p, d))
                value = terms[p, here].astype(F32)
                came(mid.at[p, 0, pl.ds(0, few)], rs1_recv.at[p, d])
                for e in reversed(order):
                    value = value + mid[p, side - e, d].astype(F32)
                mid_sum[p, d] = value.astype(BF16)
                scatter2[p][d].start()

        @pl.when(turn == 0)
        def _():
            swap_ids.wait()

        for copy in early:
            copy.wait_recv()
        ahead, _, _, _ = routing(turn + 1)
        next_route[...] = contract(ahead, early_in[routes, 0:lanes], 1, 1).astype(BF16)
        for p in range(PATHS):
            next_pre[p] = jnp.dot(ahead, early_in[p * lanes : (p + 1) * lanes, :], preferred_element_type=F32)

        for p in range(PATHS):
            sent(terms.at[p, pl.ds(0, many)], rs1_send.at[p])
        gate = gates_in[:, 0:1]
        for p in range(PATHS):
            came(landed.at[p], rs2_recv.at[p])
            result = landed[p, 0].astype(F32)
            for d in range(1, side):
                result = result + landed[p, d].astype(F32)
            value = (early_in[slots_at[p], :].astype(F32) + gate * result).astype(BF16)
            fresh[p] = value
            picked = next_pre[p] + jnp.dot(next_route[...], value, preferred_element_type=F32)

            @pl.when(turn < sections - 1)
            def _():
                chosen[p] = picked.astype(BF16)
                start_gather(p)

        @pl.when(turn < sections - 1)
        def _():
            pl.semaphore_signal(credit_landed, inc=1, device_id=below, device_id_type=MESH)

        for p in range(PATHS):
            sent(mid_sum.at[p], rs2_send.at[p])

        return carry

    lax.fori_loop(0, sections, turn_body, 0)

    for p in range(PATHS):
        final = merged(p)
        for a in range(FOLD):
            out[0, :, columns(p, a)] = final[a * n_rows : (a + 1) * n_rows, :]
    for copy in early:
        copy.wait_send()


def body(sections, side, acts, norm_gain, router, w_gate, w_up, w_down, expert_ids):
    chips = side * side
    n_rows, depth = acts.shape[1], acts.shape[2]
    part = depth // PATHS
    width = part // FOLD
    hid = w_gate.shape[2]
    lanes = FOLD * n_rows
    block = FOLD * CAP
    total = chips * block
    taken = chips * CAP
    router = jnp.transpose(router, (0, 2, 1))
    expert_ids = jnp.transpose(expert_ids, (0, 1, 3, 2))
    hbm = pl.BlockSpec(memory_space=pl.ANY)
    dma = pltpu.SemaphoreType.DMA
    return pl.pallas_call(
        functools.partial(relay_kernel, sections, side),
        out_shape=jax.ShapeDtypeStruct(acts.shape, acts.dtype),
        in_specs=[hbm] * 7,
        out_specs=pl.BlockSpec(memory_space=pltpu.VMEM),
        scratch_shapes=[
            pltpu.VMEM(acts.shape, BF16),
            pltpu.VMEM(norm_gain.shape, F32),
            pltpu.VMEM(router.shape, BF16),
            pltpu.VMEM((2, *expert_ids.shape[1:]), jnp.int32),
            pltpu.VMEM((2, depth, hid), BF16),
            pltpu.VMEM((2, depth, hid), BF16),
            pltpu.VMEM((2 * hid, depth), BF16),
            pltpu.VMEM((PATHS, chips, block, width), BF16),
            pltpu.VMEM((PATHS, chips, block, width), BF16),
            pltpu.VMEM((PATHS, side, side, block, width), BF16),
            pltpu.VMEM((PATHS, side, block, width), BF16),
            pltpu.VMEM((PATHS, side, block, width), BF16),
            pltpu.VMEM((PATHS, lanes, width), BF16),
            pltpu.VMEM((PATHS, block, width), BF16),
            pltpu.VMEM((PATHS * (lanes + block) + block, width), BF16),
            pltpu.VMEM((PATHS * (lanes + block) + block, width), BF16),
            pltpu.VMEM((PATHS, block, width), BF16),
            pltpu.VMEM((taken, part), BF16),
            pltpu.VMEM((taken, 4 * hid), F32),
            pltpu.VMEM((taken, 2 * hid), BF16),
            pltpu.VMEM((total, width), BF16),
            pltpu.VMEM((total, total), BF16),
            pltpu.VMEM((total, total), BF16),
            pltpu.VMEM((PATHS, block, width), F32),
            pltpu.VMEM((block, block), BF16),
            pltpu.VMEM((PATHS, block, width), F32),
            pltpu.VMEM((block, 128), F32),
            pltpu.VMEM((block, 128), F32),
            dma((4,)), dma((5,)), dma((6,)), dma((6,)),
            dma((PATHS,)), dma((PATHS, side - 1)), dma((PATHS,)),
            dma((PATHS,)), dma((PATHS, side)), dma((PATHS,)), dma((PATHS,)),
            dma((2,)), dma((2,)),
            pltpu.SemaphoreType.REGULAR, pltpu.SemaphoreType.REGULAR,
        ],
        compiler_params=pltpu.CompilerParams(
            collective_id=0, has_side_effects=True, vmem_limit_bytes=56 * 2**20
        ),
        name="relay",
    )(acts, norm_gain, router, w_gate, w_up, w_down, expert_ids)


def solution(mesh):
    sections, et = mesh.shape["section"], mesh.shape["et"]
    side = math.isqrt(et // 2)
    return jax.shard_map(
        functools.partial(body, sections, side),
        mesh=mesh,
        in_specs=(
            P("section", "et", None),
            P("section", None),
            P("section", None, None),
            P("section", None, "et"),
            P("section", None, "et"),
            P("section", "et", None),
            P("section", None, "et", None),
        ),
        out_specs=P("section", "et", None),
        check_vma=False,
    )
```

```python
import functools
import math

import jax
import jax.numpy as jnp
from jax import lax
from jax.experimental import pallas as pl
from jax.experimental.pallas import tpu as pltpu
from jax.sharding import PartitionSpec as P

MESH = pl.DeviceIdType.MESH
F32 = jnp.float32
BF16 = jnp.bfloat16
CAP = 4
FOLD = 4
PATHS = 2
EPS = 1e-05


def iota(shape, dim):
    return lax.broadcasted_iota(jnp.int32, shape, dim)


def contract(a, b, dim_a, dim_b):
    return lax.dot_general(a, b, (((dim_a,), (dim_b,)), ((), ())), preferred_element_type=F32)


def far_first(side):
    return sorted(range(1, side), key=lambda d: (-min(d, side - d), d))


def relay_kernel(
    sections, side, acts_hbm, gain_hbm, router_hbm, w_gate, w_up, w_down, ids_hbm, out,
    acts, gain, router, ids,
    wg, wu, wd, gathered, terms, mid, mid_sum, landed, rows, chosen, early_out, early_in, fresh,
    sums_gu, perm, perm_back, gain_fold, next_route, next_pre, gates_out, gates_in,
    in_sem, w_local, w_send, w_recv, ag_send, ag1_recv, ag2_recv,
    rs1_send, rs1_recv, rs2_send, rs2_recv, z_send, z_recv, credit_early, credit_landed,
):
    chips = side * side
    n_rows, depth = acts.shape[1], acts.shape[2]
    part = depth // PATHS
    width = part // FOLD
    hid = w_down.shape[1]
    lanes = FOLD * n_rows
    block = FOLD * CAP
    total = chips * block
    taken = chips * CAP

    section = lax.axis_index("section")
    et = lax.axis_index("et")
    core = lax.rem(et, 2)
    chip = et // 2
    cx = chip // side
    cy = lax.rem(chip, side)

    def chip_at(dx, dy):
        return lax.rem(cx + dx, side) * side + lax.rem(cy + dy, side)

    def device_at(dx, dy):
        return (section, chip_at(dx, dy) * 2 + core)

    def steps(p, d, e=0):
        turned = lax.rem(p + core, 2)
        return d + turned * (e - d), e + turned * (d - e)

    order = far_first(side)
    sibling = (section, chip * 2 + 1 - core)
    next_section = lax.rem(section + 1, sections)
    last_section = lax.rem(section + sections - 1, sections)
    above = (next_section, chip * 2 + 1 - core)
    below = (last_section, chip * 2 + 1 - core)

    barrier = pltpu.get_barrier_semaphore()
    partners = [sibling, above, below]
    for axis in range(2):
        for d in order:
            there = chip_at(*((d, 0) if axis == 0 else (0, d))) * 2
            partners += [
                (section, there + core), (next_section, there + 1 - core), (last_section, there + 1 - core)
            ]
    for device in partners:
        pl.semaphore_signal(barrier, inc=1, device_id=device, device_id_type=MESH)

    inputs = [
        pltpu.make_async_copy(src, dst, in_sem.at[i])
        for i, (src, dst) in enumerate(
            ((acts_hbm, acts), (ids_hbm.at[0], ids.at[0]), (gain_hbm, gain), (router_hbm, router))
        )
    ]
    for copy in inputs:
        copy.start()
    pieces = []
    for p in range(PATHS):
        for src, dst in ((w_gate, wg), (w_up, wu)):
            span = pl.ds(p * part, part)
            pieces.append((src.at[0, span], dst.at[0, span], dst.at[1, span]))
    pieces.append((w_down.at[0], wd.at[pl.ds(0, hid)], wd.at[pl.ds(hid, hid)]))
    loads = [pltpu.make_async_copy(src, dst, w_local.at[i]) for i, (src, dst, _) in enumerate(pieces)]
    for load in loads:
        load.start()

    def routing(turn):
        batch = lax.rem(section - turn + 2 * sections, sections)
        both = ids[lax.rem(turn, 2), batch].astype(F32).astype(BF16)
        tile = jnp.where(iota((n_rows, lanes), 0) == lax.rem(iota((n_rows, lanes), 1), n_rows), 1.0, 0.0)
        lane_ids = jnp.dot(both, tile.astype(BF16), preferred_element_type=F32)
        first, second = lane_ids[0:1, :], lane_ids[1:2, :]
        held = jnp.where((first == 0.0) | (second == 0.0), 1.0, 0.0) * (turn <= section).astype(F32)
        other = (first + second) * held
        i = iota((lanes, lanes), 0)
        j = iota((lanes, lanes), 1)
        upto = jnp.where((i // n_rows == j // n_rows) & (i <= j), 1.0, 0.0).astype(BF16)
        spots = jnp.dot(jnp.broadcast_to(held, (8, lanes)).astype(BF16), upto, preferred_element_type=F32)
        spot = spots[0:1, :] - 1.0
        keep = jnp.where((i == j) & (held == 0.0), 1.0, 0.0).astype(BF16)
        i = iota((block, lanes), 0)
        j = iota((block, lanes), 1)
        match = (i // CAP == j // n_rows) & (lax.rem(i, CAP).astype(F32) == spot) & (held > 0.0)
        select = jnp.where(match, 1.0, 0.0)
        rival = jnp.sum(select * other, axis=1, keepdims=True)
        valid = jnp.sum(select, axis=1, keepdims=True)
        return select.astype(BF16), rival, valid, keep

    i = iota((total, total), 0)
    j = iota((total, total), 1)
    source = lax.rem(i, taken) // CAP * block + i // taken * CAP + lax.rem(i, CAP)
    perm[...] = jnp.where(j == source, 1.0, 0.0).astype(BF16)
    source = lax.rem(i, block) // CAP * taken + i // block * CAP + lax.rem(i, CAP)
    perm_back[...] = jnp.where(j == source, 1.0, 0.0).astype(BF16)
    fold_of = iota((block, 1), 0) // CAP

    def columns(p, a):
        return slice(p * part + a * width, p * part + (a + 1) * width)

    inputs[0].wait()
    inputs[1].wait()
    select, _, _, _ = routing(0)
    for p in range(PATHS):
        for a in range(FOLD):
            rows[p, a * n_rows : (a + 1) * n_rows, :] = acts[0, :, columns(p, a)]
        chosen[p] = jnp.dot(select, rows[p], preferred_element_type=F32).astype(BF16)

    pl.semaphore_wait(barrier, len(partners))

    def remote(src, dst, send, recv, device):
        return pltpu.make_async_remote_copy(
            src_ref=src, dst_ref=dst, send_sem=send, recv_sem=recv, device_id=device, device_id_type=MESH
        )

    def own_chip(p, d):
        return chip_at(*steps(p, side - d)) if d else chip

    gather1 = [
        {
            d: remote(
                chosen.at[p], gathered.at[p, chip], ag_send.at[p], ag1_recv.at[p, d - 1],
                device_at(*steps(p, d)),
            )
            for d in order
        }
        for p in range(PATHS)
    ]
    gather2 = [
        {
            (d, e): remote(
                chosen.at[p] if d == 0 else gathered.at[p, own_chip(p, d)],
                gathered.at[p, own_chip(p, d)],
                ag_send.at[p], ag2_recv.at[p],
                device_at(*steps(p, 0, e)),
            )
            for d in range(side)
            for e in order
        }
        for p in range(PATHS)
    ]
    scatter1 = [
        {
            (d, e): remote(
                terms.at[p, chip_at(*steps(p, d, e))],
                mid.at[p, side - e, d],
                rs1_send.at[p], rs1_recv.at[p, d],
                device_at(*steps(p, 0, e)),
            )
            for d in range(side)
            for e in order
        }
        for p in range(PATHS)
    ]
    scatter2 = [
        {
            d: remote(
                mid_sum.at[p, d], landed.at[p, (side - d) % side], rs2_send.at[p], rs2_recv.at[p],
                (next_section, chip_at(*steps(p, d)) * 2 + 1 - core),
            )
            for d in range(side)
        }
        for p in range(PATHS)
    ]
    early = [
        remote(early_out, early_in, z_send.at[0], z_recv.at[0], above),
        remote(gates_out, gates_in, z_send.at[1], z_recv.at[1], above),
    ]
    swap_ids = remote(ids.at[0], ids.at[1], w_send.at[len(pieces)], w_recv.at[len(pieces)], sibling)
    few, many = side - 1, side * (side - 1)

    def sent(ref, sem):
        remote(ref, ref, sem, sem, sibling).wait_send()

    def came(ref, sem):
        remote(ref, ref, sem, sem, sibling).wait_recv()

    swaps = [remote(src, dst, w_send.at[i], w_recv.at[i], sibling) for i, (src, _, dst) in enumerate(pieces)]

    def start_gather(p):
        for d in order:
            gather1[p][d].start()
        for e in order:
            gather2[p][0, e].start()
        gathered[p, chip] = chosen[p]

    routes = slice(PATHS * lanes, PATHS * lanes + block)
    slots_at = [slice(routes.stop + p * block, routes.stop + (p + 1) * block) for p in range(PATHS)]

    def merged(p):
        incoming = contract(early_in[routes, 0:lanes], fresh[p], 0, 0)
        return (early_in[p * lanes : (p + 1) * lanes, :].astype(F32) + incoming).astype(BF16)

    for p in range(PATHS):
        start_gather(p)
    swap_ids.start()
    for swap in swaps:
        swap.start()

    inputs[2].wait()
    inputs[3].wait()
    for p in range(PATHS):
        folded = jnp.zeros((block, width), F32)
        for a in range(FOLD):
            folded = jnp.where(fold_of == a, gain[0:1, columns(p, a)], folded)
        gain_fold[p] = folded

    def turn_body(turn, carry):
        for p in range(PATHS):
            if p == PATHS - 1:

                @pl.when(turn > 0)
                def _():
                    pl.semaphore_wait(credit_landed, 1)

            for d in reversed(order):
                gather1[p][d].wait_recv()
                for e in order:
                    gather2[p][d, e].start()

        @pl.when(turn > 0)
        def _():
            for p in range(PATHS):
                rows[p] = merged(p)
            pl.semaphore_signal(credit_early, inc=1, device_id=below, device_id_type=MESH)

        select, rival, valid, keep = routing(turn)

        partial = jnp.zeros((block, router.shape[1]), F32)
        square = jnp.zeros((block, 1), F32)
        for p in range(PATHS):
            x = chosen[p].astype(F32)
            weighted = (x * gain_fold[p]).astype(BF16)
            square = square + jnp.sum(x * x, axis=1, keepdims=True)
            for a in range(FOLD):
                piece = contract(weighted, router[0, :, columns(p, a)], 1, 1)
                partial = partial + jnp.where(fold_of == a, piece, 0.0)
        logits = jnp.zeros_like(partial)
        squares = jnp.zeros_like(square)
        row_slot = lax.rem(iota((block, 1), 0), CAP)
        for slot in range(CAP):
            here = row_slot == slot
            logits = jnp.where(here, jnp.sum(jnp.where(here, partial, 0.0), axis=0, keepdims=True), logits)
            squares = jnp.where(here, jnp.sum(jnp.where(here, square, 0.0), axis=0, keepdims=True), squares)
        logits = logits * lax.rsqrt(squares / depth + EPS)
        expert = iota(logits.shape, 1).astype(F32)
        l_rival = jnp.sum(jnp.where(expert == rival, logits, 0.0), axis=1, keepdims=True)
        gate = valid * jax.nn.sigmoid(logits[:, 0:1] - l_rival)

        @pl.when(turn > 0)
        def _():
            for copy in early:
                copy.wait_send()

        for p in range(PATHS):
            early_out[p * lanes : (p + 1) * lanes, :] = jnp.dot(
                keep, rows[p], preferred_element_type=F32
            ).astype(BF16)
            early_out[slots_at[p], :] = chosen[p]
        early_out[routes, 0:lanes] = select
        gates_out[...] = jnp.broadcast_to(gate, gates_out.shape)

        @pl.when(turn > 0)
        def _():
            pl.semaphore_wait(credit_early, 1)

        for copy in early:
            copy.start()

        square = jnp.zeros((taken, 1), F32)
        for p in range(PATHS):
            came(gathered.at[p, pl.ds(0, many)], ag2_recv.at[p])

            @pl.when(turn == 0)
            def _():
                for n in (2 * p, 2 * p + 1):
                    loads[n].wait()
                    swaps[n].wait()

            everyone = gathered[p].reshape(total, width)
            ordered = jnp.dot(perm[...], everyone, preferred_element_type=F32)
            dots = [0.0] * 4
            for a in range(FOLD):
                piece = ordered[a * taken : (a + 1) * taken, :]
                square = square + jnp.sum(piece * piece, axis=1, keepdims=True)
                piece = (piece * gain[0:1, columns(p, a)]).astype(BF16)
                for n, w in enumerate((wg.at[0], wg.at[1], wu.at[0], wu.at[1])):
                    dots[n] = dots[n] + jnp.dot(piece, w[columns(p, a), :], preferred_element_type=F32)
            if p == 0:
                for n in range(4):
                    sums_gu[:, n * hid : (n + 1) * hid] = dots[n]
        scale = lax.rsqrt(square / depth + EPS)
        dots = [dots[n] + sums_gu[:, n * hid : (n + 1) * hid] for n in range(4)]
        hidden = jnp.concatenate(
            [(jax.nn.silu(dots[half] * scale) * (dots[2 + half] * scale)).astype(BF16) for half in range(2)], axis=1
        )

        @pl.when(turn == 0)
        def _():
            loads[4].wait()
            swaps[4].wait()

        for p in range(PATHS):
            stacked = jnp.concatenate(
                [
                    jnp.dot(hidden, wd[:, columns(p, a)], preferred_element_type=F32).astype(BF16)
                    for a in range(FOLD)
                ],
                axis=0,
            )
            reordered = jnp.dot(perm_back[...], stacked, preferred_element_type=F32)
            terms[p] = reordered.astype(BF16).reshape(chips, block, width)
            if p == 0:
                for q in range(PATHS):
                    sent(gathered.at[q, pl.ds(0, few + many)], ag_send.at[q])
            for d in (*order, 0):
                for e in order:
                    scatter1[p][d, e].start()

        def look_ahead():
            for copy in early:
                copy.wait_recv()
            ahead, _, _, _ = routing(turn + 1)
            next_route[...] = contract(ahead, early_in[routes, 0:lanes], 1, 1).astype(BF16)
            for p in range(PATHS):
                next_pre[p] = jnp.dot(ahead, early_in[p * lanes : (p + 1) * lanes, :], preferred_element_type=F32)

        def pass_up(p, d):
            here = chip_at(*steps(p, d))
            value = terms[p, here].astype(F32)
            came(mid.at[p, 0, pl.ds(0, few)], rs1_recv.at[p, d])
            for e in reversed(order):
                value = value + mid[p, side - e, d].astype(F32)
            mid_sum[p, d] = value.astype(BF16)
            scatter2[p][d].start()

        def take_in(p):
            came(landed.at[p], rs2_recv.at[p])
            result = landed[p, 0].astype(F32)
            for d in range(1, side):
                result = result + landed[p, d].astype(F32)
            value = (early_in[slots_at[p], :].astype(F32) + gates_in[:, 0:1] * result).astype(BF16)
            fresh[p] = value
            picked = next_pre[p] + jnp.dot(next_route[...], value, preferred_element_type=F32)

            @pl.when(turn < sections - 1)
            def _():
                chosen[p] = picked.astype(BF16)
                start_gather(p)

        @pl.when(turn == 0)
        def _():
            swap_ids.wait()

        look_ahead()
        for p in range(PATHS):
            for d in (*order, 0):
                pass_up(p, d)
        for p in range(PATHS):
            take_in(p)

        @pl.when(turn < sections - 1)
        def _():
            pl.semaphore_signal(credit_landed, inc=1, device_id=below, device_id_type=MESH)

        for p in range(PATHS):
            sent(terms.at[p, pl.ds(0, many)], rs1_send.at[p])
            sent(mid_sum.at[p], rs2_send.at[p])

        return carry

    lax.fori_loop(0, sections, turn_body, 0)

    for p in range(PATHS):
        final = merged(p)
        for a in range(FOLD):
            out[0, :, columns(p, a)] = final[a * n_rows : (a + 1) * n_rows, :]
    for copy in early:
        copy.wait_send()


def body(sections, side, acts, norm_gain, router, w_gate, w_up, w_down, expert_ids):
    chips = side * side
    n_rows, depth = acts.shape[1], acts.shape[2]
    part = depth // PATHS
    width = part // FOLD
    hid = w_gate.shape[2]
    lanes = FOLD * n_rows
    block = FOLD * CAP
    total = chips * block
    taken = chips * CAP
    router = jnp.transpose(router, (0, 2, 1))
    expert_ids = jnp.transpose(expert_ids, (0, 1, 3, 2))
    hbm = pl.BlockSpec(memory_space=pl.ANY)
    dma = pltpu.SemaphoreType.DMA
    return pl.pallas_call(
        functools.partial(relay_kernel, sections, side),
        out_shape=jax.ShapeDtypeStruct(acts.shape, acts.dtype),
        in_specs=[hbm] * 7,
        out_specs=pl.BlockSpec(memory_space=pltpu.VMEM),
        scratch_shapes=[
            pltpu.VMEM(acts.shape, BF16),
            pltpu.VMEM(norm_gain.shape, F32),
            pltpu.VMEM(router.shape, BF16),
            pltpu.VMEM((2, *expert_ids.shape[1:]), jnp.int32),
            pltpu.VMEM((2, depth, hid), BF16),
            pltpu.VMEM((2, depth, hid), BF16),
            pltpu.VMEM((2 * hid, depth), BF16),
            pltpu.VMEM((PATHS, chips, block, width), BF16),
            pltpu.VMEM((PATHS, chips, block, width), BF16),
            pltpu.VMEM((PATHS, side, side, block, width), BF16),
            pltpu.VMEM((PATHS, side, block, width), BF16),
            pltpu.VMEM((PATHS, side, block, width), BF16),
            pltpu.VMEM((PATHS, lanes, width), BF16),
            pltpu.VMEM((PATHS, block, width), BF16),
            pltpu.VMEM((PATHS * (lanes + block) + block, width), BF16),
            pltpu.VMEM((PATHS * (lanes + block) + block, width), BF16),
            pltpu.VMEM((PATHS, block, width), BF16),
            pltpu.VMEM((taken, 4 * hid), F32),
            pltpu.VMEM((total, total), BF16),
            pltpu.VMEM((total, total), BF16),
            pltpu.VMEM((PATHS, block, width), F32),
            pltpu.VMEM((block, block), BF16),
            pltpu.VMEM((PATHS, block, width), F32),
            pltpu.VMEM((block, 128), F32),
            pltpu.VMEM((block, 128), F32),
            dma((4,)), dma((5,)), dma((6,)), dma((6,)),
            dma((PATHS,)), dma((PATHS, side - 1)), dma((PATHS,)),
            dma((PATHS,)), dma((PATHS, side)), dma((PATHS,)), dma((PATHS,)),
            dma((2,)), dma((2,)),
            pltpu.SemaphoreType.REGULAR, pltpu.SemaphoreType.REGULAR,
        ],
        compiler_params=pltpu.CompilerParams(
            collective_id=0, has_side_effects=True, vmem_limit_bytes=56 * 2**20
        ),
        name="relay",
    )(acts, norm_gain, router, w_gate, w_up, w_down, expert_ids)


def solution(mesh):
    sections, et = mesh.shape["section"], mesh.shape["et"]
    side = math.isqrt(et // 2)
    return jax.shard_map(
        functools.partial(body, sections, side),
        mesh=mesh,
        in_specs=(
            P("section", "et", None),
            P("section", None),
            P("section", None, None),
            P("section", None, "et"),
            P("section", None, "et"),
            P("section", "et", None),
            P("section", None, "et", None),
        ),
        out_specs=P("section", "et", None),
        check_vma=False,
    )
```

```python
import functools
import math

import jax
import jax.numpy as jnp
from jax import lax
from jax.experimental import pallas as pl
from jax.experimental.pallas import tpu as pltpu
from jax.sharding import PartitionSpec as P

MESH = pl.DeviceIdType.MESH
F32 = jnp.float32
BF16 = jnp.bfloat16
CAP = 4
FOLD = 4
PATHS = 2
EPS = 1e-05


def iota(shape, dim):
    return lax.broadcasted_iota(jnp.int32, shape, dim)


def contract(a, b, dim_a, dim_b):
    return lax.dot_general(a, b, (((dim_a,), (dim_b,)), ((), ())), preferred_element_type=F32)


def far_first(side):
    return sorted(range(1, side), key=lambda d: (-min(d, side - d), d))


def relay_kernel(
    sections, side, acts_hbm, gain_hbm, router_hbm, w_gate, w_up, w_down, ids_hbm, out,
    acts, gain, router, ids,
    wg, wu, wd, gathered, terms, mid, mid_sum, landed, rows, chosen, early_out, early_in, fresh,
    sums_gu, perm, perm_back, gain_fold, next_route, next_pre, gates_out, gates_in,
    in_sem, w_local, w_send, w_recv, ag_send, ag1_recv, ag2_recv,
    rs1_send, rs1_recv, rs2_send, rs2_recv, z_send, z_recv, credit_early, credit_landed,
):
    chips = side * side
    n_rows, depth = acts.shape[1], acts.shape[2]
    part = depth // PATHS
    width = part // FOLD
    hid = w_down.shape[1]
    lanes = FOLD * n_rows
    block = FOLD * CAP
    total = chips * block
    taken = chips * CAP

    section = lax.axis_index("section")
    et = lax.axis_index("et")
    core = lax.rem(et, 2)
    chip = et // 2
    cx = chip // side
    cy = lax.rem(chip, side)

    def chip_at(dx, dy):
        return lax.rem(cx + dx, side) * side + lax.rem(cy + dy, side)

    def device_at(dx, dy):
        return (section, chip_at(dx, dy) * 2 + core)

    def steps(p, d, e=0):
        turned = lax.rem(p + core, 2)
        return d + turned * (e - d), e + turned * (d - e)

    order = far_first(side)
    sibling = (section, chip * 2 + 1 - core)
    next_section = lax.rem(section + 1, sections)
    last_section = lax.rem(section + sections - 1, sections)
    above = (next_section, chip * 2 + 1 - core)
    below = (last_section, chip * 2 + 1 - core)

    barrier = pltpu.get_barrier_semaphore()
    partners = [sibling, above]
    senders = [below]
    for axis in range(2):
        for d in order:
            there = chip_at(*((d, 0) if axis == 0 else (0, d))) * 2
            partners += [(section, there + core), (next_section, there + 1 - core)]
            senders.append((last_section, there + 1 - core))
    partners += senders
    for device in partners:
        pl.semaphore_signal(barrier, inc=1, device_id=device, device_id_type=MESH)

    inputs = [
        pltpu.make_async_copy(src, dst, in_sem.at[i])
        for i, (src, dst) in enumerate(
            ((acts_hbm, acts), (ids_hbm.at[0], ids.at[0]), (gain_hbm, gain), (router_hbm, router))
        )
    ]
    for copy in inputs:
        copy.start()
    pieces = []
    for p in range(PATHS):
        for src, dst in ((w_gate, wg), (w_up, wu)):
            span = pl.ds(p * part, part)
            pieces.append((src.at[0, span], dst.at[0, span], dst.at[1, span]))
    for p in range(PATHS):
        span = pl.ds(p * part, part)
        pieces.append((w_down.at[0, :, span], wd.at[pl.ds(0, hid), span], wd.at[pl.ds(hid, hid), span]))
    loads = [pltpu.make_async_copy(src, dst, w_local.at[i]) for i, (src, dst, _) in enumerate(pieces)]
    for load in loads:
        load.start()

    def routing(turn):
        batch = lax.rem(section - turn + 2 * sections, sections)
        both = ids[lax.rem(turn, 2), batch].astype(F32).astype(BF16)
        tile = jnp.where(iota((n_rows, lanes), 0) == lax.rem(iota((n_rows, lanes), 1), n_rows), 1.0, 0.0)
        lane_ids = jnp.dot(both, tile.astype(BF16), preferred_element_type=F32)
        first, second = lane_ids[0:1, :], lane_ids[1:2, :]
        held = jnp.where((first == 0.0) | (second == 0.0), 1.0, 0.0) * (turn <= section).astype(F32)
        other = (first + second) * held
        i = iota((lanes, lanes), 0)
        j = iota((lanes, lanes), 1)
        upto = jnp.where((i // n_rows == j // n_rows) & (i <= j), 1.0, 0.0).astype(BF16)
        spots = jnp.dot(jnp.broadcast_to(held, (8, lanes)).astype(BF16), upto, preferred_element_type=F32)
        spot = spots[0:1, :] - 1.0
        keep = jnp.where((i == j) & (held == 0.0), 1.0, 0.0).astype(BF16)
        i = iota((block, lanes), 0)
        j = iota((block, lanes), 1)
        match = (i // CAP == j // n_rows) & (lax.rem(i, CAP).astype(F32) == spot) & (held > 0.0)
        select = jnp.where(match, 1.0, 0.0)
        rival = jnp.sum(select * other, axis=1, keepdims=True)
        valid = jnp.sum(select, axis=1, keepdims=True)
        return select.astype(BF16), rival, valid, keep

    i = iota((total, total), 0)
    j = iota((total, total), 1)
    source = lax.rem(i, taken) // CAP * block + i // taken * CAP + lax.rem(i, CAP)
    perm[...] = jnp.where(j == source, 1.0, 0.0).astype(BF16)
    source = lax.rem(i, block) // CAP * taken + i // block * CAP + lax.rem(i, CAP)
    perm_back[...] = jnp.where(j == source, 1.0, 0.0).astype(BF16)
    fold_of = iota((block, 1), 0) // CAP

    def columns(p, a):
        return slice(p * part + a * width, p * part + (a + 1) * width)

    inputs[0].wait()
    inputs[1].wait()
    select, _, _, _ = routing(0)
    for p in range(PATHS):
        for a in range(FOLD):
            rows[p, a * n_rows : (a + 1) * n_rows, :] = acts[0, :, columns(p, a)]
        chosen[p] = jnp.dot(select, rows[p], preferred_element_type=F32).astype(BF16)

    pl.semaphore_wait(barrier, len(partners))

    def remote(src, dst, send, recv, device):
        return pltpu.make_async_remote_copy(
            src_ref=src, dst_ref=dst, send_sem=send, recv_sem=recv, device_id=device, device_id_type=MESH
        )

    def own_chip(p, d):
        return chip_at(*steps(p, side - d)) if d else chip

    gather1 = [
        {
            d: remote(
                chosen.at[p], gathered.at[p, chip], ag_send.at[p], ag1_recv.at[p, d - 1],
                device_at(*steps(p, d)),
            )
            for d in order
        }
        for p in range(PATHS)
    ]
    gather2 = [
        {
            (d, e): remote(
                chosen.at[p] if d == 0 else gathered.at[p, own_chip(p, d)],
                gathered.at[p, own_chip(p, d)],
                ag_send.at[p], ag2_recv.at[p],
                device_at(*steps(p, 0, e)),
            )
            for d in range(side)
            for e in order
        }
        for p in range(PATHS)
    ]
    scatter1 = [
        {
            (d, e): remote(
                terms.at[p, chip_at(*steps(p, d, e))],
                mid.at[p, side - e, d],
                rs1_send.at[p], rs1_recv.at[p, d],
                device_at(*steps(p, 0, e)),
            )
            for d in range(side)
            for e in order
        }
        for p in range(PATHS)
    ]
    scatter2 = [
        {
            d: remote(
                mid_sum.at[p, d], landed.at[p, (side - d) % side], rs2_send.at[p], rs2_recv.at[p],
                (next_section, chip_at(*steps(p, d)) * 2 + 1 - core),
            )
            for d in range(side)
        }
        for p in range(PATHS)
    ]

    def early(slot):
        return [
            remote(early_out, early_in.at[slot], z_send.at[0], z_recv.at[slot, 0], above),
            remote(gates_out, gates_in.at[slot], z_send.at[1], z_recv.at[slot, 1], above),
        ]

    swap_ids = remote(ids.at[0], ids.at[1], w_send.at[len(pieces)], w_recv.at[len(pieces)], sibling)
    few, many = side - 1, side * (side - 1)

    def sent(ref, sem):
        remote(ref, ref, sem, sem, sibling).wait_send()

    def came(ref, sem):
        remote(ref, ref, sem, sem, sibling).wait_recv()

    swaps = [remote(src, dst, w_send.at[i], w_recv.at[i], sibling) for i, (src, _, dst) in enumerate(pieces)]

    def start_gather(p):
        for d in order:
            gather1[p][d].start()
        for e in order:
            gather2[p][0, e].start()
        gathered[p, chip] = chosen[p]

    routes = slice(PATHS * lanes, PATHS * lanes + block)
    slots_at = [slice(routes.stop + p * block, routes.stop + (p + 1) * block) for p in range(PATHS)]

    def merged(slot, p):
        incoming = contract(early_in[slot, routes, 0:lanes], fresh[p], 0, 0)
        return (early_in[slot, p * lanes : (p + 1) * lanes, :].astype(F32) + incoming).astype(BF16)

    for p in range(PATHS):
        start_gather(p)
    swap_ids.start()
    for swap in swaps:
        swap.start()

    inputs[2].wait()
    inputs[3].wait()
    for p in range(PATHS):
        folded = jnp.zeros((block, width), F32)
        for a in range(FOLD):
            folded = jnp.where(fold_of == a, gain[0:1, columns(p, a)], folded)
        gain_fold[p] = folded

    def turn_body(turn, carry):
        now, before = lax.rem(turn, 2), lax.rem(turn + 1, 2)

        for p in range(PATHS):
            for d in reversed(order):
                gather1[p][d].wait_recv()
                for e in order:
                    gather2[p][d, e].start()

        @pl.when(turn > 0)
        def _():
            for p in range(PATHS):
                rows[p] = merged(before, p)
            for device in senders:
                pl.semaphore_signal(credit_landed, inc=1, device_id=device, device_id_type=MESH)

        @pl.when((turn > 0) & (turn < sections - 1))
        def _():
            pl.semaphore_signal(credit_early, inc=1, device_id=below, device_id_type=MESH)

        select, rival, valid, keep = routing(turn)

        partial = jnp.zeros((block, router.shape[1]), F32)
        square = jnp.zeros((block, 1), F32)
        for p in range(PATHS):
            x = chosen[p].astype(F32)
            weighted = (x * gain_fold[p]).astype(BF16)
            square = square + jnp.sum(x * x, axis=1, keepdims=True)
            for a in range(FOLD):
                piece = contract(weighted, router[0, :, columns(p, a)], 1, 1)
                partial = partial + jnp.where(fold_of == a, piece, 0.0)
        logits = jnp.zeros_like(partial)
        squares = jnp.zeros_like(square)
        row_slot = lax.rem(iota((block, 1), 0), CAP)
        for slot in range(CAP):
            here = row_slot == slot
            logits = jnp.where(here, jnp.sum(jnp.where(here, partial, 0.0), axis=0, keepdims=True), logits)
            squares = jnp.where(here, jnp.sum(jnp.where(here, square, 0.0), axis=0, keepdims=True), squares)
        logits = logits * lax.rsqrt(squares / depth + EPS)
        expert = iota(logits.shape, 1).astype(F32)
        l_rival = jnp.sum(jnp.where(expert == rival, logits, 0.0), axis=1, keepdims=True)
        gate = valid * jax.nn.sigmoid(logits[:, 0:1] - l_rival)

        @pl.when(turn > 0)
        def _():
            for copy in early(before):
                copy.wait_send()

        for p in range(PATHS):
            early_out[p * lanes : (p + 1) * lanes, :] = jnp.dot(
                keep, rows[p], preferred_element_type=F32
            ).astype(BF16)
            early_out[slots_at[p], :] = chosen[p]
        early_out[routes, 0:lanes] = select
        gates_out[...] = jnp.broadcast_to(gate, gates_out.shape)

        @pl.when(turn > 1)
        def _():
            pl.semaphore_wait(credit_early, 1)

        for copy in early(now):
            copy.start()

        square = jnp.zeros((taken, 1), F32)
        for p in range(PATHS):
            came(gathered.at[p, pl.ds(0, many)], ag2_recv.at[p])

            @pl.when(turn == 0)
            def _():
                for n in (2 * p, 2 * p + 1):
                    loads[n].wait()
                    swaps[n].wait()

            everyone = gathered[p].reshape(total, width)
            ordered = jnp.dot(perm[...], everyone, preferred_element_type=F32)
            dots = [0.0] * 4
            for a in range(FOLD):
                piece = ordered[a * taken : (a + 1) * taken, :]
                square = square + jnp.sum(piece * piece, axis=1, keepdims=True)
                piece = (piece * gain[0:1, columns(p, a)]).astype(BF16)
                for n, w in enumerate((wg.at[0], wg.at[1], wu.at[0], wu.at[1])):
                    dots[n] = dots[n] + jnp.dot(piece, w[columns(p, a), :], preferred_element_type=F32)
            if p == 0:
                for n in range(4):
                    sums_gu[:, n * hid : (n + 1) * hid] = dots[n]
        scale = lax.rsqrt(square / depth + EPS)
        dots = [dots[n] + sums_gu[:, n * hid : (n + 1) * hid] for n in range(4)]
        hidden = jnp.concatenate(
            [(jax.nn.silu(dots[half] * scale) * (dots[2 + half] * scale)).astype(BF16) for half in range(2)], axis=1
        )

        for p in range(PATHS):

            @pl.when(turn == 0)
            def _():
                loads[4 + p].wait()
                swaps[4 + p].wait()

            stacked = jnp.concatenate(
                [
                    jnp.dot(hidden, wd[:, columns(p, a)], preferred_element_type=F32).astype(BF16)
                    for a in range(FOLD)
                ],
                axis=0,
            )
            reordered = jnp.dot(perm_back[...], stacked, preferred_element_type=F32)
            terms[p] = reordered.astype(BF16).reshape(chips, block, width)
            if p == 0:
                for q in range(PATHS):
                    sent(gathered.at[q, pl.ds(0, few + many)], ag_send.at[q])
            for d in (*order, 0):
                for e in order:
                    scatter1[p][d, e].start()

        def look_ahead():
            for copy in early(now):
                copy.wait_recv()
            ahead, _, _, _ = routing(turn + 1)
            next_route[...] = contract(ahead, early_in[now, routes, 0:lanes], 1, 1).astype(BF16)
            for p in range(PATHS):
                held_over = early_in[now, p * lanes : (p + 1) * lanes, :]
                next_pre[p] = jnp.dot(ahead, held_over, preferred_element_type=F32)

        def pass_up(p, d):
            here = chip_at(*steps(p, d))
            value = terms[p, here].astype(F32)
            came(mid.at[p, 0, pl.ds(0, few)], rs1_recv.at[p, d])
            for e in reversed(order):
                value = value + mid[p, side - e, d].astype(F32)
            mid_sum[p, d] = value.astype(BF16)
            scatter2[p][d].start()

        def take_in(p):
            came(landed.at[p], rs2_recv.at[p])
            result = landed[p, 0].astype(F32)
            for d in range(1, side):
                result = result + landed[p, d].astype(F32)
            value = (early_in[now, slots_at[p], :].astype(F32) + gates_in[now, :, 0:1] * result).astype(BF16)
            fresh[p] = value
            picked = next_pre[p] + jnp.dot(next_route[...], value, preferred_element_type=F32)

            @pl.when(turn < sections - 1)
            def _():
                chosen[p] = picked.astype(BF16)
                start_gather(p)

        @pl.when(turn == 0)
        def _():
            swap_ids.wait()

        @pl.when(turn > 0)
        def _():
            pl.semaphore_wait(credit_landed, len(senders))

        groups = (*order, 0)
        for p in range(PATHS):
            for n, d in enumerate(groups):
                pass_up(p, d)
                if p == 0 and n == 1:
                    look_ahead()
        for p in range(PATHS):
            take_in(p)

        for p in range(PATHS):
            sent(terms.at[p, pl.ds(0, many)], rs1_send.at[p])
            sent(mid_sum.at[p], rs2_send.at[p])

        return carry

    lax.fori_loop(0, sections, turn_body, 0)

    for p in range(PATHS):
        final = merged((sections - 1) % 2, p)
        for a in range(FOLD):
            out[0, :, columns(p, a)] = final[a * n_rows : (a + 1) * n_rows, :]
    for copy in early((sections - 1) % 2):
        copy.wait_send()


def body(sections, side, acts, norm_gain, router, w_gate, w_up, w_down, expert_ids):
    chips = side * side
    n_rows, depth = acts.shape[1], acts.shape[2]
    part = depth // PATHS
    width = part // FOLD
    hid = w_gate.shape[2]
    lanes = FOLD * n_rows
    block = FOLD * CAP
    total = chips * block
    taken = chips * CAP
    router = jnp.transpose(router, (0, 2, 1))
    expert_ids = jnp.transpose(expert_ids, (0, 1, 3, 2))
    hbm = pl.BlockSpec(memory_space=pl.ANY)
    dma = pltpu.SemaphoreType.DMA
    return pl.pallas_call(
        functools.partial(relay_kernel, sections, side),
        out_shape=jax.ShapeDtypeStruct(acts.shape, acts.dtype),
        in_specs=[hbm] * 7,
        out_specs=pl.BlockSpec(memory_space=pltpu.VMEM),
        scratch_shapes=[
            pltpu.VMEM(acts.shape, BF16),
            pltpu.VMEM(norm_gain.shape, F32),
            pltpu.VMEM(router.shape, BF16),
            pltpu.VMEM((2, *expert_ids.shape[1:]), jnp.int32),
            pltpu.VMEM((2, depth, hid), BF16),
            pltpu.VMEM((2, depth, hid), BF16),
            pltpu.VMEM((2 * hid, depth), BF16),
            pltpu.VMEM((PATHS, chips, block, width), BF16),
            pltpu.VMEM((PATHS, chips, block, width), BF16),
            pltpu.VMEM((PATHS, side, side, block, width), BF16),
            pltpu.VMEM((PATHS, side, block, width), BF16),
            pltpu.VMEM((PATHS, side, block, width), BF16),
            pltpu.VMEM((PATHS, lanes, width), BF16),
            pltpu.VMEM((PATHS, block, width), BF16),
            pltpu.VMEM((PATHS * (lanes + block) + block, width), BF16),
            pltpu.VMEM((2, PATHS * (lanes + block) + block, width), BF16),
            pltpu.VMEM((PATHS, block, width), BF16),
            pltpu.VMEM((taken, 4 * hid), F32),
            pltpu.VMEM((total, total), BF16),
            pltpu.VMEM((total, total), BF16),
            pltpu.VMEM((PATHS, block, width), F32),
            pltpu.VMEM((block, block), BF16),
            pltpu.VMEM((PATHS, block, width), F32),
            pltpu.VMEM((block, 128), F32),
            pltpu.VMEM((2, block, 128), F32),
            dma((4,)), dma((6,)), dma((7,)), dma((7,)),
            dma((PATHS,)), dma((PATHS, side - 1)), dma((PATHS,)),
            dma((PATHS,)), dma((PATHS, side)), dma((PATHS,)), dma((PATHS,)),
            dma((2,)), dma((2, 2)),
            pltpu.SemaphoreType.REGULAR, pltpu.SemaphoreType.REGULAR,
        ],
        compiler_params=pltpu.CompilerParams(
            collective_id=0, has_side_effects=True, vmem_limit_bytes=56 * 2**20
        ),
        name="relay",
    )(acts, norm_gain, router, w_gate, w_up, w_down, expert_ids)


def solution(mesh):
    sections, et = mesh.shape["section"], mesh.shape["et"]
    side = math.isqrt(et // 2)
    return jax.shard_map(
        functools.partial(body, sections, side),
        mesh=mesh,
        in_specs=(
            P("section", "et", None),
            P("section", None),
            P("section", None, None),
            P("section", None, "et"),
            P("section", None, "et"),
            P("section", "et", None),
            P("section", None, "et", None),
        ),
        out_specs=P("section", "et", None),
        check_vma=False,
    )
```

```python
import functools
import math

import jax
import jax.numpy as jnp
from jax import lax
from jax.experimental import pallas as pl
from jax.experimental.pallas import tpu as pltpu
from jax.sharding import PartitionSpec as P

MESH = pl.DeviceIdType.MESH
F32 = jnp.float32
BF16 = jnp.bfloat16
CAP = 4
FOLD = 4
PATHS = 2
EPS = 1e-05


def iota(shape, dim):
    return lax.broadcasted_iota(jnp.int32, shape, dim)


def contract(a, b, dim_a, dim_b):
    return lax.dot_general(a, b, (((dim_a,), (dim_b,)), ((), ())), preferred_element_type=F32)


def far_first(side):
    return sorted(range(1, side), key=lambda d: (-min(d, side - d), d))


def relay_kernel(
    sections, side, acts_hbm, gain_hbm, router_hbm, w_gate, w_up, w_down, ids_hbm, out,
    acts, gain, router, ids,
    wg, wu, wd, gathered, terms, mid, mid_sum, landed, rows, chosen, early_out, early_in, fresh,
    sums_gu, perm, perm_back, gain_fold, next_route, next_pre, gates_out, gates_in,
    in_sem, w_local, w_send, w_recv, ag_send, ag1_recv, ag2_recv,
    rs1_send, rs1_recv, rs2_send, rs2_recv, z_send, z_recv, credit_early, credit_landed,
):
    chips = side * side
    n_rows, depth = acts.shape[1], acts.shape[2]
    part = depth // PATHS
    width = part // FOLD
    hid = w_down.shape[1]
    lanes = FOLD * n_rows
    block = FOLD * CAP
    total = chips * block
    taken = chips * CAP

    section = lax.axis_index("section")
    et = lax.axis_index("et")
    core = lax.rem(et, 2)
    chip = et // 2
    cx = chip // side
    cy = lax.rem(chip, side)

    def chip_at(dx, dy):
        return lax.rem(cx + dx, side) * side + lax.rem(cy + dy, side)

    def device_at(dx, dy):
        return (section, chip_at(dx, dy) * 2 + core)

    def steps(p, d, e=0):
        turned = lax.rem(p + core, 2)
        return d + turned * (e - d), e + turned * (d - e)

    order = far_first(side)
    sibling = (section, chip * 2 + 1 - core)
    next_section = lax.rem(section + 1, sections)
    last_section = lax.rem(section + sections - 1, sections)
    above = (next_section, chip * 2 + 1 - core)
    below = (last_section, chip * 2 + 1 - core)

    barrier = pltpu.get_barrier_semaphore()
    partners = [sibling, above]
    senders = [below]
    for axis in range(2):
        for d in order:
            there = chip_at(*((d, 0) if axis == 0 else (0, d))) * 2
            partners += [(section, there + core), (next_section, there + 1 - core)]
            senders.append((last_section, there + 1 - core))
    partners += senders
    for device in partners:
        pl.semaphore_signal(barrier, inc=1, device_id=device, device_id_type=MESH)

    inputs = [
        pltpu.make_async_copy(src, dst, in_sem.at[i])
        for i, (src, dst) in enumerate(
            ((acts_hbm, acts), (ids_hbm.at[0], ids.at[0]), (gain_hbm, gain), (router_hbm, router))
        )
    ]
    for copy in inputs:
        copy.start()
    pieces = []
    for p in range(PATHS):
        for src, dst in ((w_gate, wg), (w_up, wu)):
            span = pl.ds(p * part, part)
            pieces.append((src.at[0, span], dst.at[0, span], dst.at[1, span]))
    for p in range(PATHS):
        span = pl.ds(p * part, part)
        pieces.append((w_down.at[0, :, span], wd.at[pl.ds(0, hid), span], wd.at[pl.ds(hid, hid), span]))
    loads = [pltpu.make_async_copy(src, dst, w_local.at[i]) for i, (src, dst, _) in enumerate(pieces)]
    for load in loads:
        load.start()

    def routing(turn):
        batch = lax.rem(section - turn + 2 * sections, sections)
        both = ids[lax.rem(turn, 2), batch].astype(F32).astype(BF16)
        tile = jnp.where(iota((n_rows, lanes), 0) == lax.rem(iota((n_rows, lanes), 1), n_rows), 1.0, 0.0)
        lane_ids = jnp.dot(both, tile.astype(BF16), preferred_element_type=F32)
        first, second = lane_ids[0:1, :], lane_ids[1:2, :]
        held = jnp.where((first == 0.0) | (second == 0.0), 1.0, 0.0) * (turn <= section).astype(F32)
        other = (first + second) * held
        i = iota((lanes, lanes), 0)
        j = iota((lanes, lanes), 1)
        upto = jnp.where((i // n_rows == j // n_rows) & (i <= j), 1.0, 0.0).astype(BF16)
        spots = jnp.dot(jnp.broadcast_to(held, (8, lanes)).astype(BF16), upto, preferred_element_type=F32)
        spot = spots[0:1, :] - 1.0
        keep = jnp.where((i == j) & (held == 0.0), 1.0, 0.0).astype(BF16)
        i = iota((block, lanes), 0)
        j = iota((block, lanes), 1)
        match = (i // CAP == j // n_rows) & (lax.rem(i, CAP).astype(F32) == spot) & (held > 0.0)
        select = jnp.where(match, 1.0, 0.0)
        rival = jnp.sum(select * other, axis=1, keepdims=True)
        valid = jnp.sum(select, axis=1, keepdims=True)
        return select.astype(BF16), rival, valid, keep

    i = iota((total, total), 0)
    j = iota((total, total), 1)
    source = lax.rem(i, taken) // CAP * block + i // taken * CAP + lax.rem(i, CAP)
    perm[...] = jnp.where(j == source, 1.0, 0.0).astype(BF16)
    source = lax.rem(i, block) // CAP * taken + i // block * CAP + lax.rem(i, CAP)
    perm_back[...] = jnp.where(j == source, 1.0, 0.0).astype(BF16)
    fold_of = iota((block, 1), 0) // CAP

    def columns(p, a):
        return slice(p * part + a * width, p * part + (a + 1) * width)

    inputs[0].wait()
    inputs[1].wait()
    select, _, _, _ = routing(0)
    for p in range(PATHS):
        for a in range(FOLD):
            rows[p, a * n_rows : (a + 1) * n_rows, :] = acts[0, :, columns(p, a)]
        chosen[p] = jnp.dot(select, rows[p], preferred_element_type=F32).astype(BF16)

    pl.semaphore_wait(barrier, len(partners))

    def remote(src, dst, send, recv, device):
        return pltpu.make_async_remote_copy(
            src_ref=src, dst_ref=dst, send_sem=send, recv_sem=recv, device_id=device, device_id_type=MESH
        )

    def own_chip(p, d):
        return chip_at(*steps(p, side - d)) if d else chip

    gather1 = [
        {
            d: remote(
                chosen.at[p], gathered.at[p, chip], ag_send.at[p], ag1_recv.at[p, d - 1],
                device_at(*steps(p, d)),
            )
            for d in order
        }
        for p in range(PATHS)
    ]
    gather2 = [
        {
            (d, e): remote(
                chosen.at[p] if d == 0 else gathered.at[p, own_chip(p, d)],
                gathered.at[p, own_chip(p, d)],
                ag_send.at[p], ag2_recv.at[p],
                device_at(*steps(p, 0, e)),
            )
            for d in range(side)
            for e in order
        }
        for p in range(PATHS)
    ]
    scatter1 = [
        {
            (d, e): remote(
                terms.at[p, chip_at(*steps(p, d, e))],
                mid.at[p, side - e, d],
                rs1_send.at[p], rs1_recv.at[p, d],
                device_at(*steps(p, 0, e)),
            )
            for d in range(side)
            for e in order
        }
        for p in range(PATHS)
    ]
    scatter2 = [
        {
            d: remote(
                mid_sum.at[p, d], landed.at[p, (side - d) % side], rs2_send.at[p], rs2_recv.at[p],
                (next_section, chip_at(*steps(p, d)) * 2 + 1 - core),
            )
            for d in range(side)
        }
        for p in range(PATHS)
    ]

    def early(slot):
        return [
            remote(early_out, early_in.at[slot], z_send.at[0], z_recv.at[slot, 0], above),
            remote(gates_out, gates_in.at[slot], z_send.at[1], z_recv.at[slot, 1], above),
        ]

    swap_ids = remote(ids.at[0], ids.at[1], w_send.at[len(pieces)], w_recv.at[len(pieces)], sibling)
    few, many = side - 1, side * (side - 1)

    def sent(ref, sem):
        remote(ref, ref, sem, sem, sibling).wait_send()

    def came(ref, sem):
        remote(ref, ref, sem, sem, sibling).wait_recv()

    swaps = [remote(src, dst, w_send.at[i], w_recv.at[i], sibling) for i, (src, _, dst) in enumerate(pieces)]

    def start_gather(p):
        for d in order:
            gather1[p][d].start()
        for e in order:
            gather2[p][0, e].start()
        gathered[p, chip] = chosen[p]

    routes = slice(PATHS * lanes, PATHS * lanes + block)
    slots_at = [slice(routes.stop + p * block, routes.stop + (p + 1) * block) for p in range(PATHS)]

    def merged(slot, p):
        incoming = contract(early_in[slot, routes, 0:lanes], fresh[p], 0, 0)
        return (early_in[slot, p * lanes : (p + 1) * lanes, :].astype(F32) + incoming).astype(BF16)

    for p in range(PATHS):
        start_gather(p)
    swap_ids.start()
    for swap in swaps:
        swap.start()

    inputs[2].wait()
    inputs[3].wait()
    for p in range(PATHS):
        folded = jnp.zeros((block, width), F32)
        for a in range(FOLD):
            folded = jnp.where(fold_of == a, gain[0:1, columns(p, a)], folded)
        gain_fold[p] = folded

    def turn_body(turn, carry):
        now, before = lax.rem(turn, 2), lax.rem(turn + 1, 2)

        for p in range(PATHS):
            for d in reversed(order):
                gather1[p][d].wait_recv()
                gather2[p][d, order[0]].start()
            for d in reversed(order):
                for e in order[1:]:
                    gather2[p][d, e].start()

        @pl.when(turn > 0)
        def _():
            for p in range(PATHS):
                rows[p] = merged(before, p)
            for device in senders:
                pl.semaphore_signal(credit_landed, inc=1, device_id=device, device_id_type=MESH)

        @pl.when((turn > 0) & (turn < sections - 1))
        def _():
            pl.semaphore_signal(credit_early, inc=1, device_id=below, device_id_type=MESH)

        select, rival, valid, keep = routing(turn)

        partial = jnp.zeros((block, router.shape[1]), F32)
        square = jnp.zeros((block, 1), F32)
        for p in range(PATHS):
            x = chosen[p].astype(F32)
            weighted = (x * gain_fold[p]).astype(BF16)
            square = square + jnp.sum(x * x, axis=1, keepdims=True)
            for a in range(FOLD):
                piece = contract(weighted, router[0, :, columns(p, a)], 1, 1)
                partial = partial + jnp.where(fold_of == a, piece, 0.0)
        logits = jnp.zeros_like(partial)
        squares = jnp.zeros_like(square)
        row_slot = lax.rem(iota((block, 1), 0), CAP)
        for slot in range(CAP):
            here = row_slot == slot
            logits = jnp.where(here, jnp.sum(jnp.where(here, partial, 0.0), axis=0, keepdims=True), logits)
            squares = jnp.where(here, jnp.sum(jnp.where(here, square, 0.0), axis=0, keepdims=True), squares)
        logits = logits * lax.rsqrt(squares / depth + EPS)
        expert = iota(logits.shape, 1).astype(F32)
        l_rival = jnp.sum(jnp.where(expert == rival, logits, 0.0), axis=1, keepdims=True)
        gate = valid * jax.nn.sigmoid(logits[:, 0:1] - l_rival)

        @pl.when(turn > 0)
        def _():
            for copy in early(before):
                copy.wait_send()

        for p in range(PATHS):
            early_out[p * lanes : (p + 1) * lanes, :] = jnp.dot(
                keep, rows[p], preferred_element_type=F32
            ).astype(BF16)
            early_out[slots_at[p], :] = chosen[p]
        early_out[routes, 0:lanes] = select
        gates_out[...] = jnp.broadcast_to(gate, gates_out.shape)

        @pl.when(turn > 1)
        def _():
            pl.semaphore_wait(credit_early, 1)

        for copy in early(now):
            copy.start()

        square = jnp.zeros((taken, 1), F32)
        for p in range(PATHS):
            came(gathered.at[p, pl.ds(0, many)], ag2_recv.at[p])

            @pl.when(turn == 0)
            def _():
                for n in (2 * p, 2 * p + 1):
                    loads[n].wait()
                    swaps[n].wait()

            everyone = gathered[p].reshape(total, width)
            ordered = jnp.dot(perm[...], everyone, preferred_element_type=F32)
            dots = [0.0] * 4
            for a in range(FOLD):
                piece = ordered[a * taken : (a + 1) * taken, :]
                square = square + jnp.sum(piece * piece, axis=1, keepdims=True)
                piece = (piece * gain[0:1, columns(p, a)]).astype(BF16)
                for n, w in enumerate((wg.at[0], wg.at[1], wu.at[0], wu.at[1])):
                    dots[n] = dots[n] + jnp.dot(piece, w[columns(p, a), :], preferred_element_type=F32)
            if p == 0:
                for n in range(4):
                    sums_gu[:, n * hid : (n + 1) * hid] = dots[n]
        scale = lax.rsqrt(square / depth + EPS)
        dots = [dots[n] + sums_gu[:, n * hid : (n + 1) * hid] for n in range(4)]
        hidden = jnp.concatenate(
            [(jax.nn.silu(dots[half] * scale) * (dots[2 + half] * scale)).astype(BF16) for half in range(2)], axis=1
        )

        for p in range(PATHS):

            @pl.when(turn == 0)
            def _():
                loads[4 + p].wait()
                swaps[4 + p].wait()

            stacked = jnp.concatenate(
                [
                    jnp.dot(hidden, wd[:, columns(p, a)], preferred_element_type=F32).astype(BF16)
                    for a in range(FOLD)
                ],
                axis=0,
            )
            reordered = jnp.dot(perm_back[...], stacked, preferred_element_type=F32)
            terms[p] = reordered.astype(BF16).reshape(chips, block, width)
            if p == 0:
                for q in range(PATHS):
                    sent(gathered.at[q, pl.ds(0, few + many)], ag_send.at[q])
            for d in (*order, 0):
                for e in order:
                    scatter1[p][d, e].start()

        def look_ahead():
            for copy in early(now):
                copy.wait_recv()
            ahead, _, _, _ = routing(turn + 1)
            next_route[...] = contract(ahead, early_in[now, routes, 0:lanes], 1, 1).astype(BF16)
            for p in range(PATHS):
                held_over = early_in[now, p * lanes : (p + 1) * lanes, :]
                next_pre[p] = jnp.dot(ahead, held_over, preferred_element_type=F32)

        def pass_up(p, d):
            here = chip_at(*steps(p, d))
            value = terms[p, here].astype(F32)
            came(mid.at[p, 0, pl.ds(0, few)], rs1_recv.at[p, d])
            for e in reversed(order):
                value = value + mid[p, side - e, d].astype(F32)
            mid_sum[p, d] = value.astype(BF16)
            scatter2[p][d].start()

        def take_in(p):
            came(landed.at[p], rs2_recv.at[p])
            result = landed[p, 0].astype(F32)
            for d in range(1, side):
                result = result + landed[p, d].astype(F32)
            value = (early_in[now, slots_at[p], :].astype(F32) + gates_in[now, :, 0:1] * result).astype(BF16)
            fresh[p] = value
            picked = next_pre[p] + jnp.dot(next_route[...], value, preferred_element_type=F32)

            @pl.when(turn < sections - 1)
            def _():
                chosen[p] = picked.astype(BF16)
                start_gather(p)

        @pl.when(turn == 0)
        def _():
            swap_ids.wait()

        @pl.when(turn > 0)
        def _():
            pl.semaphore_wait(credit_landed, len(senders))

        groups = (*order, 0)
        for p in range(PATHS):
            for n, d in enumerate(groups):
                pass_up(p, d)
                if p == 0 and n == 1:
                    look_ahead()
        for p in range(PATHS):
            take_in(p)

        for p in range(PATHS):
            sent(terms.at[p, pl.ds(0, many)], rs1_send.at[p])
            sent(mid_sum.at[p], rs2_send.at[p])

        return carry

    lax.fori_loop(0, sections, turn_body, 0)

    for p in range(PATHS):
        final = merged((sections - 1) % 2, p)
        for a in range(FOLD):
            out[0, :, columns(p, a)] = final[a * n_rows : (a + 1) * n_rows, :]
    for copy in early((sections - 1) % 2):
        copy.wait_send()


def body(sections, side, acts, norm_gain, router, w_gate, w_up, w_down, expert_ids):
    chips = side * side
    n_rows, depth = acts.shape[1], acts.shape[2]
    part = depth // PATHS
    width = part // FOLD
    hid = w_gate.shape[2]
    lanes = FOLD * n_rows
    block = FOLD * CAP
    total = chips * block
    taken = chips * CAP
    router = jnp.transpose(router, (0, 2, 1))
    expert_ids = jnp.transpose(expert_ids, (0, 1, 3, 2))
    hbm = pl.BlockSpec(memory_space=pl.ANY)
    dma = pltpu.SemaphoreType.DMA
    return pl.pallas_call(
        functools.partial(relay_kernel, sections, side),
        out_shape=jax.ShapeDtypeStruct(acts.shape, acts.dtype),
        in_specs=[hbm] * 7,
        out_specs=pl.BlockSpec(memory_space=pltpu.VMEM),
        scratch_shapes=[
            pltpu.VMEM(acts.shape, BF16),
            pltpu.VMEM(norm_gain.shape, F32),
            pltpu.VMEM(router.shape, BF16),
            pltpu.VMEM((2, *expert_ids.shape[1:]), jnp.int32),
            pltpu.VMEM((2, depth, hid), BF16),
            pltpu.VMEM((2, depth, hid), BF16),
            pltpu.VMEM((2 * hid, depth), BF16),
            pltpu.VMEM((PATHS, chips, block, width), BF16),
            pltpu.VMEM((PATHS, chips, block, width), BF16),
            pltpu.VMEM((PATHS, side, side, block, width), BF16),
            pltpu.VMEM((PATHS, side, block, width), BF16),
            pltpu.VMEM((PATHS, side, block, width), BF16),
            pltpu.VMEM((PATHS, lanes, width), BF16),
            pltpu.VMEM((PATHS, block, width), BF16),
            pltpu.VMEM((PATHS * (lanes + block) + block, width), BF16),
            pltpu.VMEM((2, PATHS * (lanes + block) + block, width), BF16),
            pltpu.VMEM((PATHS, block, width), BF16),
            pltpu.VMEM((taken, 4 * hid), F32),
            pltpu.VMEM((total, total), BF16),
            pltpu.VMEM((total, total), BF16),
            pltpu.VMEM((PATHS, block, width), F32),
            pltpu.VMEM((block, block), BF16),
            pltpu.VMEM((PATHS, block, width), F32),
            pltpu.VMEM((block, 128), F32),
            pltpu.VMEM((2, block, 128), F32),
            dma((4,)), dma((6,)), dma((7,)), dma((7,)),
            dma((PATHS,)), dma((PATHS, side - 1)), dma((PATHS,)),
            dma((PATHS,)), dma((PATHS, side)), dma((PATHS,)), dma((PATHS,)),
            dma((2,)), dma((2, 2)),
            pltpu.SemaphoreType.REGULAR, pltpu.SemaphoreType.REGULAR,
        ],
        compiler_params=pltpu.CompilerParams(
            collective_id=0, has_side_effects=True, vmem_limit_bytes=56 * 2**20
        ),
        name="relay",
    )(acts, norm_gain, router, w_gate, w_up, w_down, expert_ids)


def solution(mesh):
    sections, et = mesh.shape["section"], mesh.shape["et"]
    side = math.isqrt(et // 2)
    return jax.shard_map(
        functools.partial(body, sections, side),
        mesh=mesh,
        in_specs=(
            P("section", "et", None),
            P("section", None),
            P("section", None, None),
            P("section", None, "et"),
            P("section", None, "et"),
            P("section", "et", None),
            P("section", None, "et", None),
        ),
        out_specs=P("section", "et", None),
        check_vma=False,
    )
```

```python
import functools
import math

import jax
import jax.numpy as jnp
from jax import lax
from jax.experimental import pallas as pl
from jax.experimental.pallas import tpu as pltpu
from jax.sharding import PartitionSpec as P

MESH = pl.DeviceIdType.MESH
F32 = jnp.float32
BF16 = jnp.bfloat16
CAP = 4
FOLD = 4
PATHS = 2
EPS = 1e-05


def iota(shape, dim):
    return lax.broadcasted_iota(jnp.int32, shape, dim)


def contract(a, b, dim_a, dim_b):
    return lax.dot_general(a, b, (((dim_a,), (dim_b,)), ((), ())), preferred_element_type=F32)


def far_first(side):
    return sorted(range(1, side), key=lambda d: (-min(d, side - d), d))


def relay_kernel(
    sections, side, acts_hbm, gain_hbm, router_hbm, w_gate, w_up, w_down, ids_hbm, out,
    acts, gain, router, ids,
    wg, wu, wd, gathered, terms, mid, mid_sum, landed, rows, chosen, early_out, early_in, fresh,
    sums_gu, perm, perm_back, gain_fold, next_route, next_pre, gates_out, gates_in,
    in_sem, w_local, w_send, w_recv, ag_send, ag1_recv, ag2_recv,
    rs1_send, rs1_recv, rs2_send, rs2_recv, z_send, z_recv, credit_early, credit_landed,
):
    chips = side * side
    n_rows, depth = acts.shape[1], acts.shape[2]
    part = depth // PATHS
    width = part // FOLD
    hid = w_down.shape[1]
    lanes = FOLD * n_rows
    block = FOLD * CAP
    total = chips * block
    taken = chips * CAP

    section = lax.axis_index("section")
    et = lax.axis_index("et")
    core = lax.rem(et, 2)
    chip = et // 2
    cx = chip // side
    cy = lax.rem(chip, side)

    def chip_at(dx, dy):
        return lax.rem(cx + dx, side) * side + lax.rem(cy + dy, side)

    def device_at(dx, dy):
        return (section, chip_at(dx, dy) * 2 + core)

    def steps(p, d, e=0):
        turned = lax.rem(p + core, 2)
        return d + turned * (e - d), e + turned * (d - e)

    order = far_first(side)
    sibling = (section, chip * 2 + 1 - core)
    next_section = lax.rem(section + 1, sections)
    last_section = lax.rem(section + sections - 1, sections)
    above = (next_section, chip * 2 + 1 - core)
    below = (last_section, chip * 2 + 1 - core)

    barrier = pltpu.get_barrier_semaphore()
    partners = [sibling, above]
    senders = [below]
    for axis in range(2):
        for d in order:
            there = chip_at(*((d, 0) if axis == 0 else (0, d))) * 2
            partners += [(section, there + core), (next_section, there + 1 - core)]
            senders.append((last_section, there + 1 - core))
    partners += senders
    for device in partners:
        pl.semaphore_signal(barrier, inc=1, device_id=device, device_id_type=MESH)

    inputs = [
        pltpu.make_async_copy(src, dst, in_sem.at[i])
        for i, (src, dst) in enumerate(
            ((acts_hbm, acts), (ids_hbm.at[0], ids.at[0]), (gain_hbm, gain), (router_hbm, router))
        )
    ]
    for copy in inputs:
        copy.start()
    pieces = []
    for p in range(PATHS):
        for src, dst in ((w_gate, wg), (w_up, wu)):
            span = pl.ds(p * part, part)
            pieces.append((src.at[0, span], dst.at[0, span], dst.at[1, span]))
    for p in range(PATHS):
        span = pl.ds(p * part, part)
        pieces.append((w_down.at[0, :, span], wd.at[pl.ds(0, hid), span], wd.at[pl.ds(hid, hid), span]))
    loads = [pltpu.make_async_copy(src, dst, w_local.at[i]) for i, (src, dst, _) in enumerate(pieces)]
    for load in loads:
        load.start()

    def routing(turn):
        batch = lax.rem(section - turn + 2 * sections, sections)
        both = ids[lax.rem(turn, 2), batch].astype(F32).astype(BF16)
        tile = jnp.where(iota((n_rows, lanes), 0) == lax.rem(iota((n_rows, lanes), 1), n_rows), 1.0, 0.0)
        lane_ids = jnp.dot(both, tile.astype(BF16), preferred_element_type=F32)
        first, second = lane_ids[0:1, :], lane_ids[1:2, :]
        held = jnp.where((first == 0.0) | (second == 0.0), 1.0, 0.0) * (turn <= section).astype(F32)
        other = (first + second) * held
        i = iota((lanes, lanes), 0)
        j = iota((lanes, lanes), 1)
        upto = jnp.where((i // n_rows == j // n_rows) & (i <= j), 1.0, 0.0).astype(BF16)
        spots = jnp.dot(jnp.broadcast_to(held, (8, lanes)).astype(BF16), upto, preferred_element_type=F32)
        spot = spots[0:1, :] - 1.0
        keep = jnp.where((i == j) & (held == 0.0), 1.0, 0.0).astype(BF16)
        i = iota((block, lanes), 0)
        j = iota((block, lanes), 1)
        match = (i // CAP == j // n_rows) & (lax.rem(i, CAP).astype(F32) == spot) & (held > 0.0)
        select = jnp.where(match, 1.0, 0.0)
        rival = jnp.sum(select * other, axis=1, keepdims=True)
        valid = jnp.sum(select, axis=1, keepdims=True)
        return select.astype(BF16), rival, valid, keep

    i = iota((total, total), 0)
    j = iota((total, total), 1)
    source = lax.rem(i, taken) // CAP * block + i // taken * CAP + lax.rem(i, CAP)
    perm[...] = jnp.where(j == source, 1.0, 0.0).astype(BF16)
    source = lax.rem(i, block) // CAP * taken + i // block * CAP + lax.rem(i, CAP)
    perm_back[...] = jnp.where(j == source, 1.0, 0.0).astype(BF16)
    fold_of = iota((block, 1), 0) // CAP

    def columns(p, a):
        return slice(p * part + a * width, p * part + (a + 1) * width)

    inputs[0].wait()
    inputs[1].wait()
    select, _, _, _ = routing(0)
    for p in range(PATHS):
        for a in range(FOLD):
            rows[p, a * n_rows : (a + 1) * n_rows, :] = acts[0, :, columns(p, a)]
        chosen[p] = jnp.dot(select, rows[p], preferred_element_type=F32).astype(BF16)

    pl.semaphore_wait(barrier, len(partners))

    def remote(src, dst, send, recv, device):
        return pltpu.make_async_remote_copy(
            src_ref=src, dst_ref=dst, send_sem=send, recv_sem=recv, device_id=device, device_id_type=MESH
        )

    def own_chip(p, d):
        return chip_at(*steps(p, side - d)) if d else chip

    gather1 = [
        {
            d: remote(
                chosen.at[p], gathered.at[p, chip], ag_send.at[p], ag1_recv.at[p, d - 1],
                device_at(*steps(p, d)),
            )
            for d in order
        }
        for p in range(PATHS)
    ]
    gather2 = [
        {
            (d, e): remote(
                chosen.at[p] if d == 0 else gathered.at[p, own_chip(p, d)],
                gathered.at[p, own_chip(p, d)],
                ag_send.at[p], ag2_recv.at[p],
                device_at(*steps(p, 0, e)),
            )
            for d in range(side)
            for e in order
        }
        for p in range(PATHS)
    ]
    scatter1 = [
        {
            (d, e): remote(
                terms.at[p, chip_at(*steps(p, d, e))],
                mid.at[p, side - e, d],
                rs1_send.at[p], rs1_recv.at[p, d],
                device_at(*steps(p, 0, e)),
            )
            for d in range(side)
            for e in order
        }
        for p in range(PATHS)
    ]
    scatter2 = [
        {
            d: remote(
                mid_sum.at[p, d], landed.at[p, (side - d) % side], rs2_send.at[p], rs2_recv.at[p],
                (next_section, chip_at(*steps(p, d)) * 2 + 1 - core),
            )
            for d in range(side)
        }
        for p in range(PATHS)
    ]

    def early(slot):
        return [
            remote(early_out, early_in.at[slot], z_send.at[0], z_recv.at[slot, 0], above),
            remote(gates_out, gates_in.at[slot], z_send.at[1], z_recv.at[slot, 1], above),
        ]

    swap_ids = remote(ids.at[0], ids.at[1], w_send.at[len(pieces)], w_recv.at[len(pieces)], sibling)
    few, many = side - 1, side * (side - 1)

    def sent(ref, sem):
        remote(ref, ref, sem, sem, sibling).wait_send()

    def came(ref, sem):
        remote(ref, ref, sem, sem, sibling).wait_recv()

    swaps = [remote(src, dst, w_send.at[i], w_recv.at[i], sibling) for i, (src, _, dst) in enumerate(pieces)]

    def start_gather(p):
        for d in order:
            gather1[p][d].start()
        for e in order:
            gather2[p][0, e].start()
        gathered[p, chip] = chosen[p]

    routes = slice(PATHS * lanes, PATHS * lanes + block)
    slots_at = [slice(routes.stop + p * block, routes.stop + (p + 1) * block) for p in range(PATHS)]

    def merged(slot, p):
        incoming = contract(early_in[slot, routes, 0:lanes], fresh[p], 0, 0)
        return (early_in[slot, p * lanes : (p + 1) * lanes, :].astype(F32) + incoming).astype(BF16)

    swap_ids.start()
    for swap in swaps:
        swap.start()
    for p in range(PATHS):
        start_gather(p)

    inputs[2].wait()
    inputs[3].wait()
    for p in range(PATHS):
        folded = jnp.zeros((block, width), F32)
        for a in range(FOLD):
            folded = jnp.where(fold_of == a, gain[0:1, columns(p, a)], folded)
        gain_fold[p] = folded

    def turn_body(turn, carry):
        now, before = lax.rem(turn, 2), lax.rem(turn + 1, 2)

        for p in range(PATHS):
            for d in reversed(order):
                gather1[p][d].wait_recv()
                for e in order:
                    gather2[p][d, e].start()

        @pl.when(turn > 0)
        def _():
            for p in range(PATHS):
                rows[p] = merged(before, p)
            for device in senders:
                pl.semaphore_signal(credit_landed, inc=1, device_id=device, device_id_type=MESH)

        @pl.when((turn > 0) & (turn < sections - 1))
        def _():
            pl.semaphore_signal(credit_early, inc=1, device_id=below, device_id_type=MESH)

        select, rival, valid, keep = routing(turn)

        partial = jnp.zeros((block, router.shape[1]), F32)
        square = jnp.zeros((block, 1), F32)
        for p in range(PATHS):
            x = chosen[p].astype(F32)
            weighted = (x * gain_fold[p]).astype(BF16)
            square = square + jnp.sum(x * x, axis=1, keepdims=True)
            for a in range(FOLD):
                piece = contract(weighted, router[0, :, columns(p, a)], 1, 1)
                partial = partial + jnp.where(fold_of == a, piece, 0.0)
        logits = jnp.zeros_like(partial)
        squares = jnp.zeros_like(square)
        row_slot = lax.rem(iota((block, 1), 0), CAP)
        for slot in range(CAP):
            here = row_slot == slot
            logits = jnp.where(here, jnp.sum(jnp.where(here, partial, 0.0), axis=0, keepdims=True), logits)
            squares = jnp.where(here, jnp.sum(jnp.where(here, square, 0.0), axis=0, keepdims=True), squares)
        logits = logits * lax.rsqrt(squares / depth + EPS)
        expert = iota(logits.shape, 1).astype(F32)
        l_rival = jnp.sum(jnp.where(expert == rival, logits, 0.0), axis=1, keepdims=True)
        gate = valid * jax.nn.sigmoid(logits[:, 0:1] - l_rival)

        @pl.when(turn > 0)
        def _():
            for copy in early(before):
                copy.wait_send()

        for p in range(PATHS):
            early_out[p * lanes : (p + 1) * lanes, :] = jnp.dot(
                keep, rows[p], preferred_element_type=F32
            ).astype(BF16)
            early_out[slots_at[p], :] = chosen[p]
        early_out[routes, 0:lanes] = select
        gates_out[...] = jnp.broadcast_to(gate, gates_out.shape)

        @pl.when(turn > 1)
        def _():
            pl.semaphore_wait(credit_early, 1)

        for copy in early(now):
            copy.start()

        square = jnp.zeros((taken, 1), F32)
        for p in range(PATHS):
            came(gathered.at[p, pl.ds(0, many)], ag2_recv.at[p])

            @pl.when(turn == 0)
            def _():
                for n in (2 * p, 2 * p + 1):
                    loads[n].wait()
                    swaps[n].wait()

            everyone = gathered[p].reshape(total, width)
            ordered = jnp.dot(perm[...], everyone, preferred_element_type=F32)
            dots = [0.0] * 4
            for a in range(FOLD):
                piece = ordered[a * taken : (a + 1) * taken, :]
                square = square + jnp.sum(piece * piece, axis=1, keepdims=True)
                piece = (piece * gain[0:1, columns(p, a)]).astype(BF16)
                for n, w in enumerate((wg.at[0], wg.at[1], wu.at[0], wu.at[1])):
                    dots[n] = dots[n] + jnp.dot(piece, w[columns(p, a), :], preferred_element_type=F32)
            if p == 0:
                for n in range(4):
                    sums_gu[:, n * hid : (n + 1) * hid] = dots[n]
        scale = lax.rsqrt(square / depth + EPS)
        dots = [dots[n] + sums_gu[:, n * hid : (n + 1) * hid] for n in range(4)]
        hidden = jnp.concatenate(
            [(jax.nn.silu(dots[half] * scale) * (dots[2 + half] * scale)).astype(BF16) for half in range(2)], axis=1
        )

        for p in range(PATHS):

            @pl.when(turn == 0)
            def _():
                loads[4 + p].wait()
                swaps[4 + p].wait()

            stacked = jnp.concatenate(
                [
                    jnp.dot(hidden, wd[:, columns(p, a)], preferred_element_type=F32).astype(BF16)
                    for a in range(FOLD)
                ],
                axis=0,
            )
            reordered = jnp.dot(perm_back[...], stacked, preferred_element_type=F32)
            terms[p] = reordered.astype(BF16).reshape(chips, block, width)
            if p == 0:
                for q in range(PATHS):
                    sent(gathered.at[q, pl.ds(0, few + many)], ag_send.at[q])
            if p == 0:
                turns = [(0, d) for d in order[:2]]
            else:
                turns = [(1, order[0]), (0, order[2]) if few > 2 else (0, 0), (1, order[-2]), (0, 0), (1, order[-1]), (1, 0)]
            for q, d in turns:
                for e in order:
                    scatter1[q][d, e].start()

        def look_ahead():
            for copy in early(now):
                copy.wait_recv()
            ahead, _, _, _ = routing(turn + 1)
            next_route[...] = contract(ahead, early_in[now, routes, 0:lanes], 1, 1).astype(BF16)
            for p in range(PATHS):
                held_over = early_in[now, p * lanes : (p + 1) * lanes, :]
                next_pre[p] = jnp.dot(ahead, held_over, preferred_element_type=F32)

        def pass_up(p, d):
            here = chip_at(*steps(p, d))
            value = terms[p, here].astype(F32)
            came(mid.at[p, 0, pl.ds(0, few)], rs1_recv.at[p, d])
            for e in reversed(order):
                value = value + mid[p, side - e, d].astype(F32)
            mid_sum[p, d] = value.astype(BF16)
            scatter2[p][d].start()

        def take_in(p):
            came(landed.at[p], rs2_recv.at[p])
            result = landed[p, 0].astype(F32)
            for d in range(1, side):
                result = result + landed[p, d].astype(F32)
            value = (early_in[now, slots_at[p], :].astype(F32) + gates_in[now, :, 0:1] * result).astype(BF16)
            fresh[p] = value
            picked = next_pre[p] + jnp.dot(next_route[...], value, preferred_element_type=F32)

            @pl.when(turn < sections - 1)
            def _():
                chosen[p] = picked.astype(BF16)
                start_gather(p)

        @pl.when(turn == 0)
        def _():
            swap_ids.wait()

        @pl.when(turn > 0)
        def _():
            pl.semaphore_wait(credit_landed, len(senders))

        groups = (*order, 0)
        for p in range(PATHS):
            for n, d in enumerate(groups):
                pass_up(p, d)
                if p == 0 and n == 1:
                    look_ahead()
        for p in range(PATHS):
            take_in(p)

        for p in range(PATHS):
            sent(terms.at[p, pl.ds(0, many)], rs1_send.at[p])
            sent(mid_sum.at[p], rs2_send.at[p])

        return carry

    lax.fori_loop(0, sections, turn_body, 0)

    for p in range(PATHS):
        final = merged((sections - 1) % 2, p)
        for a in range(FOLD):
            out[0, :, columns(p, a)] = final[a * n_rows : (a + 1) * n_rows, :]
    for copy in early((sections - 1) % 2):
        copy.wait_send()


def body(sections, side, acts, norm_gain, router, w_gate, w_up, w_down, expert_ids):
    chips = side * side
    n_rows, depth = acts.shape[1], acts.shape[2]
    part = depth // PATHS
    width = part // FOLD
    hid = w_gate.shape[2]
    lanes = FOLD * n_rows
    block = FOLD * CAP
    total = chips * block
    taken = chips * CAP
    router = jnp.transpose(router, (0, 2, 1))
    expert_ids = jnp.transpose(expert_ids, (0, 1, 3, 2))
    hbm = pl.BlockSpec(memory_space=pl.ANY)
    dma = pltpu.SemaphoreType.DMA
    return pl.pallas_call(
        functools.partial(relay_kernel, sections, side),
        out_shape=jax.ShapeDtypeStruct(acts.shape, acts.dtype),
        in_specs=[hbm] * 7,
        out_specs=pl.BlockSpec(memory_space=pltpu.VMEM),
        scratch_shapes=[
            pltpu.VMEM(acts.shape, BF16),
            pltpu.VMEM(norm_gain.shape, F32),
            pltpu.VMEM(router.shape, BF16),
            pltpu.VMEM((2, *expert_ids.shape[1:]), jnp.int32),
            pltpu.VMEM((2, depth, hid), BF16),
            pltpu.VMEM((2, depth, hid), BF16),
            pltpu.VMEM((2 * hid, depth), BF16),
            pltpu.VMEM((PATHS, chips, block, width), BF16),
            pltpu.VMEM((PATHS, chips, block, width), BF16),
            pltpu.VMEM((PATHS, side, side, block, width), BF16),
            pltpu.VMEM((PATHS, side, block, width), BF16),
            pltpu.VMEM((PATHS, side, block, width), BF16),
            pltpu.VMEM((PATHS, lanes, width), BF16),
            pltpu.VMEM((PATHS, block, width), BF16),
            pltpu.VMEM((PATHS * (lanes + block) + block, width), BF16),
            pltpu.VMEM((2, PATHS * (lanes + block) + block, width), BF16),
            pltpu.VMEM((PATHS, block, width), BF16),
            pltpu.VMEM((taken, 4 * hid), F32),
            pltpu.VMEM((total, total), BF16),
            pltpu.VMEM((total, total), BF16),
            pltpu.VMEM((PATHS, block, width), F32),
            pltpu.VMEM((block, block), BF16),
            pltpu.VMEM((PATHS, block, width), F32),
            pltpu.VMEM((block, 128), F32),
            pltpu.VMEM((2, block, 128), F32),
            dma((4,)), dma((6,)), dma((7,)), dma((7,)),
            dma((PATHS,)), dma((PATHS, side - 1)), dma((PATHS,)),
            dma((PATHS,)), dma((PATHS, side)), dma((PATHS,)), dma((PATHS,)),
            dma((2,)), dma((2, 2)),
            pltpu.SemaphoreType.REGULAR, pltpu.SemaphoreType.REGULAR,
        ],
        compiler_params=pltpu.CompilerParams(
            collective_id=0, has_side_effects=True, vmem_limit_bytes=56 * 2**20
        ),
        name="relay",
    )(acts, norm_gain, router, w_gate, w_up, w_down, expert_ids)


def solution(mesh):
    sections, et = mesh.shape["section"], mesh.shape["et"]
    side = math.isqrt(et // 2)
    return jax.shard_map(
        functools.partial(body, sections, side),
        mesh=mesh,
        in_specs=(
            P("section", "et", None),
            P("section", None),
            P("section", None, None),
            P("section", None, "et"),
            P("section", None, "et"),
            P("section", "et", None),
            P("section", None, "et", None),
        ),
        out_specs=P("section", "et", None),
        check_vma=False,
    )
```
